32 devices in a mesh: leaf: 4 (over y, x), rows: 8 (over z, core).
Axes of the slice: x: 2, y: 2, z: 4, core: 2. Of those that a mesh axis runs over, the one named last changes fastest.
Arguments:
- rhs_top: float32 [1, 4096, 128], P(None, 'rows'), may hold values from -6 to 6
- rhs_one: float32 [2, 2048, 128], P(None, 'rows'), may hold values from -6 to 6
- rhs_two: float32 [4, 2048, 128], P(None, 'rows'), may hold values from -6 to 6
- rhs_three: float32 [8, 1024, 128], P(None, 'rows'), may hold values from -6 to 6
- inv_top: float32 [4096, 4096], P('rows', 'leaf')
- inv_one: float32 [2048, 4096], P('rows', 'leaf')
- inv_two: float32 [2048, 8192], P('rows', 'leaf')
- inv_three: float32 [1024, 8192], P('rows', 'leaf')
- panel_one: float32 [4096, 2048], P('leaf', 'rows'), may hold values from -0.0625 to 0.0625
- panel_two: float32 [8192, 4096], P('leaf', 'rows'), may hold values from -0.0625 to 0.0625
- panel_three: float32 [8192, 4096], P('leaf', 'rows'), may hold values from -0.09375 to 0.09375
- rows_one: int32 [2, 16], P(None, 'rows'), may hold values from 0 to 31, as said below
- rows_two: int32 [4, 32], P(None, 'rows'), may hold values from 0 to 47, as said below
- rows_three: int32 [8, 32], P(None, 'rows'), may hold values from 0 to 63, as said below
Outputs:
- solution_top: float32 [1, 4096, 128], P(None, 'rows')
- solution_one: float32 [2, 2048, 128], P(None, 'rows')
- solution_two: float32 [4, 2048, 128], P(None, 'rows')
- solution_three: float32 [8, 1024, 128], P(None, 'rows')
The draws below stay inside these ranges and needn't reach their ends.
Inputs may be any that keep to these rules, and one draw needn't show every extreme that they name: `rows_one`: each row lists 16 different blocks of a chain of 32 blocks, the chain's first and last among them. `rows_two`: each row lists 32 different blocks of a chain of 48 blocks, the chain's first and last among them. `rows_three`: each row lists 32 different blocks of a chain of 64 blocks, the chain's first and last among them.
All inputs are finite; a program needn't handle non-finite values.
Results may differ from the reference program's by a relative error of at most 0.0001.
Values sent between devices are 32-bit elements; how exact they have to be, the bound alone decides.
No kernel may reach another device: no remote copies, remote signals or barrier semaphores. Data moves between devices by JAX's collectives and lax.ppermute only.
A program may use at most 128 MiB of HBM per device.

```python
import jax
import jax.numpy as jnp
from jax import lax

SEP0 = 4096
SEP1 = 2048
SEP2 = 2048
SEP3 = 1024
BLOCK = 128
K1 = 16
K2 = 32
K3 = 32
NRHS = 128


def dense_inverse(key, sep_size, sep_count):
    first_key, second_key = jax.random.split(key)
    full_shape = (sep_size, sep_count * sep_size)
    column_ids = lax.broadcasted_iota(jnp.int32, full_shape, 0)
    row_ids = lax.broadcasted_iota(jnp.int32, full_shape, 1) % sep_size
    scatter_part = jax.random.normal(first_key, full_shape, jnp.float32) / sep_size ** 0.5
    diagonal = jax.random.uniform(second_key, full_shape, jnp.float32, 0.5, 1.0)
    return scatter_part + jnp.where(row_ids == column_ids, diagonal, 0.0)


def chain_rows(key, sep_count, chain_count, listed):

    def one_row(sep_number):
        order = jax.random.permutation(jax.random.fold_in(key, sep_number), chain_count - 2) + 1
        fixed_ends = jnp.array([chain_count - 1, 0], jnp.int32)
        return jnp.concatenate([fixed_ends, order[:listed - 2].astype(jnp.int32)])
    return jax.vmap(one_row)(jnp.arange(sep_count, dtype=jnp.int32))


def draw_inv_top(key, part):
    return dense_inverse(key, SEP0, 1)


def draw_inv_one(key, part):
    return dense_inverse(key, SEP1, 2)


def draw_inv_two(key, part):
    return dense_inverse(key, SEP2, 4)


def draw_inv_three(key, part):
    return dense_inverse(key, SEP3, 8)


def draw_rows_one(key, part):
    return chain_rows(key, 2, SEP0 // BLOCK, K1)


def draw_rows_two(key, part):
    return chain_rows(key, 4, (SEP0 + SEP1) // BLOCK, K2)


def draw_rows_three(key, part):
    return chain_rows(key, 8, (SEP0 + SEP1 + SEP2) // BLOCK, K3)


def block_levels(own_key, dims, cuts, low, largest):
    def one(dim, shards_of):
        draws = jax.random.uniform(jax.random.fold_in(jax.random.fold_in(own_key, 6), dim), (shards_of,), jnp.float32, low / len(cuts), largest / len(cuts))
        return jnp.repeat(jnp.exp(draws), dims[dim] // shards_of).reshape((-1,) + (1,) * (len(dims) - dim - 1))

    loudness = one(*cuts[0])
    for cut in cuts[1:]:
        loudness = loudness * one(*cut)
    return loudness


def scatter_about(stream_key, dims, deviation, bound, cuts=(), kind=jnp.bfloat16):
    drawn = jax.random.normal(stream_key, dims, jnp.float32) * deviation
    if len(cuts) > 0:
        drawn = block_levels(stream_key, dims, cuts, -0.22, 0.18) * drawn
    return jnp.clip(drawn, min=-bound, max=bound).astype(kind)


def setup_inputs(seed: int = 0) -> dict:
    keys = jax.random.split(jax.random.key(seed), 15)
    return {
        "rhs_top": scatter_about(keys[0], (1, SEP0, NRHS), 1.0, 6.0, ((1, 8),), jnp.float32),
        "rhs_one": scatter_about(keys[1], (2, SEP1, NRHS), 1.0, 6.0, ((1, 8),), jnp.float32),
        "rhs_two": scatter_about(keys[2], (4, SEP2, NRHS), 1.0, 6.0, ((1, 8),), jnp.float32),
        "rhs_three": scatter_about(keys[3], (8, SEP3, NRHS), 1.0, 6.0, ((1, 8),), jnp.float32),
        "inv_top": draw_inv_top(jax.random.fold_in(keys[14], 71), 0),
        "inv_one": draw_inv_one(jax.random.fold_in(keys[14], 71), 0),
        "inv_two": draw_inv_two(jax.random.fold_in(keys[14], 71), 0),
        "inv_three": draw_inv_three(jax.random.fold_in(keys[14], 71), 0),
        "panel_one": scatter_about(keys[8], (2 * SEP1, K1 * BLOCK), (4 * SEP1) ** -0.5, 0.0625, ((0, 4), (1, 8)), jnp.float32),
        "panel_two": scatter_about(keys[9], (4 * SEP2, K2 * BLOCK), (4 * SEP2) ** -0.5, 0.0625, ((0, 4), (1, 8)), jnp.float32),
        "panel_three": scatter_about(keys[10], (8 * SEP3, K3 * BLOCK), (4 * SEP3) ** -0.5, 0.09375, ((0, 4), (1, 8)), jnp.float32),
        "rows_one": draw_rows_one(jax.random.fold_in(keys[14], 71), 0),
        "rows_two": draw_rows_two(jax.random.fold_in(keys[14], 71), 0),
        "rows_three": draw_rows_three(jax.random.fold_in(keys[14], 71), 0),
    }


def solve_blocks(inverse, vector, sep_count, sep_size, backward):
    blocks = inverse.reshape(sep_size, sep_count, sep_size)
    if backward:
        return jnp.einsum('cpr,prn->pcn', blocks, vector, precision=lax.Precision.HIGHEST)
    return jnp.einsum('cpr,pcn->prn', blocks, vector, precision=lax.Precision.HIGHEST)


def reference(rhs_top, rhs_one, rhs_two, rhs_three, inv_top, inv_one, inv_two, inv_three, panel_one, panel_two, panel_three, rows_one, rows_two, rows_three):
    sep_sizes = [SEP0, SEP1, SEP2, SEP3]
    sep_counts = [1, 2, 4, 8]
    right_sides = [rhs_top, rhs_one, rhs_two, rhs_three]
    inverses = [inv_top, inv_one, inv_two, inv_three]
    panels = [None, panel_one, panel_two, panel_three]
    indices = [None, rows_one, rows_two, rows_three]
    width_rhs = rhs_top.shape[2]
    owed_rows = [jnp.zeros(item.shape, jnp.float32) for item in right_sides]
    solved = [None, None, None, None]
    cut_panels = [None, None, None, None]
    all_matches = [None, None, None, None]
    for level_at in (3, 2, 1, 0):
        sep_count = sep_counts[level_at]
        sep_size = sep_sizes[level_at]
        source = right_sides[level_at] - owed_rows[level_at]
        solved[level_at] = solve_blocks(inverses[level_at], source, sep_count, sep_size, False)
        if level_at > 0:
            chain_count = sum(sep_sizes[:level_at]) // BLOCK
            width_blocks = panels[level_at].shape[1] // BLOCK
            panel_cut = panels[level_at].reshape(sep_count, sep_size, width_blocks, BLOCK)
            cut_panels[level_at] = panel_cut
            updates = jnp.einsum('pskb,psn->pkbn', panel_cut, solved[level_at], precision=lax.Precision.HIGHEST)
            matches = (jnp.arange(chain_count, dtype=jnp.int32)[None, :, None] == indices[level_at][:, None, :]).astype(jnp.float32)
            all_matches[level_at] = matches
            spread = jnp.einsum('pck,pkbn->pcbn', matches, updates, precision=lax.Precision.HIGHEST)
            owners = jnp.arange(sep_count, dtype=jnp.int32)
            offset = 0
            for upper in range(level_at):
                blocks_up = sep_sizes[upper] // BLOCK
                segment = spread[:, offset:offset + blocks_up].reshape(sep_count, sep_sizes[upper], width_rhs)
                target = (jnp.arange(sep_counts[upper], dtype=jnp.int32)[None, :] == (owners >> (level_at - upper))[:, None]).astype(jnp.float32)
                owed_rows[upper] = owed_rows[upper] + jnp.einsum('pq,prn->qrn', target, segment, precision=lax.Precision.HIGHEST)
                offset = offset + blocks_up
    results = []
    for level_at in range(4):
        sep_count = sep_counts[level_at]
        sep_size = sep_sizes[level_at]
        residue = solved[level_at]
        if level_at > 0:
            chain_count = sum(sep_sizes[:level_at]) // BLOCK
            owners = jnp.arange(sep_count, dtype=jnp.int32)
            pieces = [results[upper][owners >> (level_at - upper)] for upper in range(level_at)]
            chain_x = jnp.concatenate(pieces, axis=1).reshape(sep_count, chain_count, BLOCK, width_rhs)
            chosen = jnp.einsum('pck,pcbn->pkbn', all_matches[level_at], chain_x, precision=lax.Precision.HIGHEST)
            residue = residue - jnp.einsum('pskb,pkbn->psn', cut_panels[level_at], chosen, precision=lax.Precision.HIGHEST)
        results.append(solve_blocks(inverses[level_at], residue, sep_count, sep_size, True))
    return (results[0], results[1], results[2], results[3])
```

```python
import functools

import jax
import jax.numpy as jnp
from jax import lax
from jax.experimental import pallas as pl
from jax.experimental.pallas import tpu as pltpu
from jax.sharding import PartitionSpec as P

BLOCK = 128
F32 = jnp.float32
BF16 = jnp.bfloat16
VMEM = pl.BlockSpec(memory_space=pltpu.VMEM)
SMEM = pl.BlockSpec(memory_space=pltpu.SMEM)
LIMIT = 40 * 1024 * 1024


def cut(x):
    high = x.astype(BF16)
    return high, (x - high.astype(F32)).astype(BF16)


def wide(x):
    return jnp.concatenate(cut(x), axis=1)


def product(dims, a, xw):
    n = xw.shape[1] // 2
    high, low = cut(a)
    first = lax.dot_general(high, xw, (dims, ((), ())), preferred_element_type=F32)
    second = lax.dot_general(low, xw[:, :n], (dims, ((), ())), preferred_element_type=F32)
    return first[:, :n] + (first[:, n:] + second)


times = functools.partial(product, ((1,), (0,)))
transposed_times = functools.partial(product, ((0,), (0,)))


def tile_of(rows, largest=512):
    return min(rows, largest)


def spread_parts(meta, full, own, other, offset=0):
    rows = own[0].shape[0]
    for k in range(len(own)):
        chunk = 2 * jnp.bitwise_xor(meta[0], k)
        full[pl.ds(pl.multiple_of(offset + (chunk + meta[1]) * rows, 8), rows), :] = own[k][...]
        full[pl.ds(pl.multiple_of(offset + (chunk + 1 - meta[1]) * rows, 8), rows), :] = other[k][...]


def split_cores(meta, full, offset, keep, send):
    count, rows = keep.shape[0], keep.shape[1]
    for k in range(count):
        keep[k] = full[pl.ds(pl.multiple_of(offset + (2 * k + meta[1]) * rows, 8), rows), :]
        send[k] = full[pl.ds(pl.multiple_of(offset + (2 * k + 1 - meta[1]) * rows, 8), rows), :]


def forward_inv_kernel(owed_count, meta, rhs, *refs):
    owed, (inv, keep, send, full) = refs[:owed_count], refs[owed_count:]
    held = rhs.shape[0]
    part = inv.shape[1] // held
    tile = tile_of(part)
    for h in range(held):
        source = rhs[h]
        for item in owed:
            source = source - item[...]
        source = wide(source)
        for start in range(h * part, (h + 1) * part, tile):
            full[start : start + tile, :] = transposed_times(inv[:, start : start + tile], source)
    split_cores(meta, full, 0, keep, send)


def forward_panel_kernel(nz, has_before, cut_at, meta, rows, *refs):
    own, other, refs = refs[:nz], refs[nz : 2 * nz], refs[2 * nz :]
    if has_before:
        before, refs = refs[0], refs[1:]
    panel, keep, send, chain, full = refs
    held, listed = rows.shape
    part = panel.shape[0] // held
    tile = tile_of(part)
    spread_parts(meta, full, own, other)
    if has_before:
        chain[...] = before[: chain.shape[0], :]
    else:
        chain[...] = jnp.zeros_like(chain)
    for h in range(held):
        update = None
        for start in range(h * part, (h + 1) * part, tile):
            term = transposed_times(panel[start : start + tile, :], wide(full[start : start + tile, :]))
            update = term if update is None else update + term
        for k in range(listed):
            place = pl.ds(pl.multiple_of(rows[h, k] * BLOCK, BLOCK), BLOCK)
            chain[place, :] = chain[place, :] + update[k * BLOCK : (k + 1) * BLOCK]
    split_cores(meta, chain, cut_at, keep, send)


def backward_panel_kernel(nz, has_before, meta, rows, *refs):
    own, other, refs = refs[:nz], refs[nz : 2 * nz], refs[2 * nz :]
    offset = 0
    if has_before:
        before, refs = refs[0], refs[1:]
        offset = before.shape[0]
    panel, keep, send, chain, chosen, full = refs
    held, listed = rows.shape
    part = panel.shape[0] // held
    tile = tile_of(part)
    if has_before:
        chain[:offset, :] = before[...]
    spread_parts(meta, chain, own, other, offset)
    for h in range(held):
        for k in range(listed):
            place = pl.ds(pl.multiple_of(rows[h, k] * BLOCK, BLOCK), BLOCK)
            chosen[k * BLOCK : (k + 1) * BLOCK, :] = wide(chain[place, :])
        for start in range(h * part, (h + 1) * part, tile):
            full[start : start + tile, :] = times(panel[start : start + tile, :], chosen[...])
    split_cores(meta, full, 0, keep, send)


def backward_inv_kernel(nz, meta, *refs):
    own, other, (inv, solved, full) = refs[:nz], refs[nz : 2 * nz], refs[2 * nz :]
    held = solved.shape[0]
    part = inv.shape[1] // held
    tile = tile_of(part)
    spread_parts(meta, full, own, other)
    for h in range(held):
        total = None
        for start in range(h * part, (h + 1) * part, tile):
            term = times(inv[:, start : start + tile], wide(full[start : start + tile, :]))
            total = term if total is None else total + term
        solved[h] = total


def call(kernel, name, out_shapes, scratch, flops, smem_count, *operands):
    single = not isinstance(out_shapes, (list, tuple))
    outs = [out_shapes] if single else list(out_shapes)
    moved = sum(item.size * 4 for item in operands) + sum(item.size * 4 for item in outs)
    result = pl.pallas_call(
        kernel,
        out_shape=outs,
        in_specs=[SMEM] * smem_count + [VMEM] * (len(operands) - smem_count),
        out_specs=[VMEM] * len(outs),
        scratch_shapes=scratch,
        compiler_params=pltpu.CompilerParams(vmem_limit_bytes=LIMIT),
        cost_estimate=pl.CostEstimate(flops=flops, bytes_accessed=moved, transcendentals=0),
        name=name,
    )(*operands)
    return result[0] if single else result


def shaped(*dims):
    return jax.ShapeDtypeStruct(dims, F32)


def body(*arguments):
    rhs, inv = arguments[0:4], arguments[4:8]
    panel, index_rows = (None,) + arguments[8:11], (None,) + arguments[11:14]
    leaves, devices = lax.axis_size("leaf"), lax.axis_size("rows")
    leaf, device = lax.axis_index("leaf"), lax.axis_index("rows")
    nz = devices // 2
    z, core = device // 2, device % 2
    meta = jnp.stack([z, core]).astype(jnp.int32)
    width = rhs[0].shape[2]
    counts = [item.shape[0] for item in rhs]
    owned = [item.shape[1] for item in rhs]
    sizes = [item * devices for item in owned]
    spans = [item.shape[1] for item in inv]
    helds = [max(1, spans[l] // sizes[l]) for l in range(4)]
    groups = [max(1, sizes[l] // spans[l]) for l in range(4)]
    chunks = [item // devices for item in spans]
    offsets = [sum(sizes[:l]) for l in range(5)]

    def to_core(x):
        return lax.ppermute(x, "rows", [(r, r ^ 1) for r in range(devices)])

    def to_chip(x, k):
        return lax.ppermute(x, "rows", [(r, r ^ (2 * k)) for r in range(devices)])

    def to_leaf(x, k):
        return lax.ppermute(x, "leaf", [(i, i ^ k) for i in range(leaves)])

    def scatter_sum(keep, send):
        received = to_core(send)
        pick = lambda k: lax.dynamic_index_in_dim(keep, z ^ k, 0, False) + lax.dynamic_index_in_dim(
            received, z ^ k, 0, False
        )
        return [to_chip(pick(k), k) for k in range(nz - 1, 0, -1)] + [pick(0)]

    def gather(x):
        own = [x] + [to_chip(x, k) for k in range(1, nz)]
        return own + [to_core(item) for item in own]

    def leaf_sum(x, group):
        step = 1
        while step < group:
            x = x + to_leaf(x, step)
            step = step * 2
        return x

    def leaf_rows(x, l):
        return lax.dynamic_slice_in_dim(x, leaf * helds[l] // groups[l], helds[l], 0)

    def place(x, l):
        group, held = groups[l], helds[l]
        if leaves == group:
            return x
        out = jnp.zeros(rhs[l].shape, F32)
        for k in range(leaves // group):
            item = x if k == 0 else to_leaf(x, k * group)
            out = lax.dynamic_update_slice_in_dim(out, item, (leaf // group ^ k) * held, 0)
        return out

    def halves(rows):
        return [shaped(nz, rows, width), shaped(nz, rows, width)]

    solved = [None] * 4
    chain, owed = None, []
    for l in (3, 2, 1, 0):
        keep, send = call(
            functools.partial(forward_inv_kernel, len(owed)),
            f"forward_inv_{l}",
            halves(chunks[l]),
            [pltpu.VMEM((spans[l], width), F32)],
            6 * inv[l].size * width,
            1,
            meta,
            leaf_rows(rhs[l], l),
            *owed,
            inv[l],
        )
        solved[l] = sum(scatter_sum(keep, send)[::-1])
        if l == 0:
            break
        parts = gather(solved[l])
        before = [] if chain is None else [chain]
        keep, send, chain = call(
            functools.partial(forward_panel_kernel, nz, bool(before), offsets[l - 1]),
            f"forward_panel_{l}",
            halves(owned[l - 1]) + [shaped(offsets[l], width)],
            [pltpu.VMEM((spans[l], width), F32)],
            6 * panel[l].size * width,
            2,
            meta,
            leaf_rows(index_rows[l], l),
            *parts,
            *before,
            panel[l],
        )
        owed = scatter_sum(keep, send)
        if groups[l - 1] > 1:
            owed = [leaf_sum(sum(owed[::-1]), groups[l - 1])]
    results = []
    chain, parts = None, None
    for l in range(4):
        residue = solved[l]
        if l > 0:
            before = [] if chain is None else [chain]
            keep, send, chain = call(
                functools.partial(backward_panel_kernel, nz, bool(before)),
                f"backward_panel_{l}",
                halves(chunks[l]) + [shaped(offsets[l], width)],
                [
                    pltpu.VMEM((panel[l].shape[1], 2 * width), BF16),
                    pltpu.VMEM((spans[l], width), F32),
                ],
                6 * panel[l].size * width,
                2,
                meta,
                leaf_rows(index_rows[l], l),
                *parts,
                *before,
                panel[l],
            )
            residue = residue - sum(scatter_sum(keep, send)[::-1])
        x = call(
            functools.partial(backward_inv_kernel, nz),
            f"backward_inv_{l}",
            shaped(helds[l], owned[l], width),
            [pltpu.VMEM((spans[l], width), F32)],
            6 * inv[l].size * width,
            1,
            meta,
            *gather(residue),
            inv[l],
        )
        x = leaf_sum(x, groups[l])
        if l < 3:
            parts = gather(x[0])
        results.append(place(x, l))
    return tuple(results)


def solution(mesh):
    across = P(None, "rows", None)
    return jax.shard_map(
        body,
        mesh=mesh,
        in_specs=(across,) * 4 + (P("rows", "leaf"),) * 4 + (P("leaf", "rows"),) * 3 + (P(None, "rows"),) * 3,
        out_specs=(across,) * 4,
        check_vma=False,
    )
```

```python
import functools

import jax
import jax.numpy as jnp
from jax import lax
from jax.experimental import pallas as pl
from jax.experimental.pallas import tpu as pltpu
from jax.sharding import PartitionSpec as P

BLOCK = 128
F32 = jnp.float32
BF16 = jnp.bfloat16
VMEM = pl.BlockSpec(memory_space=pltpu.VMEM)
SMEM = pl.BlockSpec(memory_space=pltpu.SMEM)
LIMIT = 14 * 1024 * 1024


def cut(x):
    high = x.astype(BF16)
    return high, (x - high.astype(F32)).astype(BF16)


def wide(x):
    return jnp.concatenate(cut(x), axis=1)


def product(dims, a, xw):
    n = xw.shape[1] // 2
    high, low = cut(a)
    first = lax.dot_general(high, xw, (dims, ((), ())), preferred_element_type=F32)
    second = lax.dot_general(low, xw[:, :n], (dims, ((), ())), preferred_element_type=F32)
    return first[:, :n] + (first[:, n:] + second)


times = functools.partial(product, ((1,), (0,)))
transposed_times = functools.partial(product, ((0,), (0,)))


def tile_of(rows, largest=512):
    return min(rows, largest)


def spread_parts(meta, full, own, other, offset=0):
    rows = own[0].shape[0]
    for k in range(len(own)):
        chunk = 2 * jnp.bitwise_xor(meta[0], k)
        full[pl.ds(pl.multiple_of(offset + (chunk + meta[1]) * rows, 8), rows), :] = own[k][...]
        full[pl.ds(pl.multiple_of(offset + (chunk + 1 - meta[1]) * rows, 8), rows), :] = other[k][...]


def split_cores(meta, full, offset, keep, send):
    count, rows = keep.shape[0], keep.shape[1]
    for k in range(count):
        keep[k] = full[pl.ds(pl.multiple_of(offset + (2 * k + meta[1]) * rows, 8), rows), :]
        send[k] = full[pl.ds(pl.multiple_of(offset + (2 * k + 1 - meta[1]) * rows, 8), rows), :]


def forward_inv_kernel(owed_count, meta, rhs, *refs):
    owed, (inv, keep, send, full) = refs[:owed_count], refs[owed_count:]
    held = rhs.shape[0]
    part = inv.shape[1] // held
    tile = tile_of(part)
    for h in range(held):
        source = rhs[h]
        for item in owed:
            source = source - item[...]
        source = wide(source)
        for start in range(h * part, (h + 1) * part, tile):
            full[start : start + tile, :] = transposed_times(inv[:, start : start + tile], source)
    split_cores(meta, full, 0, keep, send)


def forward_top_kernel(leaves, group, meta, rhs, *refs):
    owed, (inv, keep, send, source, full) = refs[:leaves], refs[leaves:]
    rows = BLOCK // group
    source[...] = rhs[0]
    for d in range(leaves):
        place = lax.rem(jnp.bitwise_xor(meta[2], d), group) * rows
        for b in range(rhs.shape[1] // BLOCK):
            at = pl.ds(pl.multiple_of(b * BLOCK + place, 8), rows)
            source[at, :] = source[at, :] - owed[d][b * rows : (b + 1) * rows, :]
    factor = wide(source[...])
    tile = tile_of(inv.shape[1])
    for start in range(0, inv.shape[1], tile):
        full[start : start + tile, :] = transposed_times(inv[:, start : start + tile], factor)
    split_cores(meta, full, 0, keep, send)


def panel_update(panel, full, h, held):
    part = panel.shape[0] // held
    tile = tile_of(part)
    update = None
    for start in range(h * part, (h + 1) * part, tile):
        term = transposed_times(panel[start : start + tile, :], wide(full[start : start + tile, :]))
        update = term if update is None else update + term
    return update


def forward_panel_kernel(nz, before_count, cut_at, meta, rows, *refs):
    own, other, refs = refs[:nz], refs[nz : 2 * nz], refs[2 * nz :]
    before, (panel, keep, send), refs = refs[:before_count], refs[before_count : before_count + 3], refs[before_count + 3 :]
    (deferred, (chain, full)) = (refs[:-2], refs[-2:])
    held, listed = rows.shape
    spread_parts(meta, full, own, other)
    if before:
        chain[...] = before[0][...]
    else:
        chain[...] = jnp.zeros_like(chain)
    for h in range(held):
        update = panel_update(panel, full, h, held)
        for k in range(listed):
            place = pl.ds(pl.multiple_of(rows[h, k] * BLOCK, BLOCK), BLOCK)
            chain[place, :] = chain[place, :] + update[k * BLOCK : (k + 1) * BLOCK]
    split_cores(meta, chain, cut_at, keep, send)
    if len(deferred) == 2:
        split_cores(meta, chain, 0, *deferred)
    elif deferred:
        deferred[0][...] = chain[: deferred[0].shape[0], :]


def forward_last_kernel(nz, group, meta, rows, *refs):
    own, other, refs = refs[:nz], refs[nz : 2 * nz], refs[2 * nz :]
    panel, pieces, (full, update) = refs[0], refs[1:-2], refs[-2:]
    spread_parts(meta, full, own, other)
    update[...] = panel_update(panel, full, 0, 1)
    listed = rows.shape[1]
    height = BLOCK // group
    for d in range(group):
        place = jnp.bitwise_xor(lax.rem(meta[2], group), d) * height
        for k in range(listed):
            at = pl.ds(pl.multiple_of(k * BLOCK + place, 8), height)
            pieces[d][k * height : (k + 1) * height, :] = update[at, :]
        tail = pieces[d].shape[0] - listed * height
        numbers = jnp.zeros((tail, update.shape[1]), F32)
        if d == 0:
            line = lax.broadcasted_iota(jnp.int32, numbers.shape, 0)
            for k in range(listed):
                numbers = jnp.where(line == k, rows[0, k].astype(F32), numbers)
        pieces[d][listed * height :, :] = numbers


def owed_top_kernel(nz, group, listed, meta, *refs):
    parts, (deferred, owed) = refs[: 2 * nz], refs[2 * nz :]
    height = BLOCK // group
    blocks = owed.shape[0] // height
    first = (2 * meta[0] + meta[1]) * blocks
    for b in range(blocks):
        wanted = (first + b).astype(F32)
        total = jnp.zeros((height, owed.shape[1]), F32)
        for item in parts:
            for k in range(listed):
                number = item[listed * height + k : listed * height + k + 1, :]
                total = total + jnp.where(number == wanted, item[k * height : (k + 1) * height, :], 0.0)
        owed[b * height : (b + 1) * height, :] = total
    count = deferred.shape[0]
    at = pl.ds(pl.multiple_of((meta[2] // group) * count, 8), count)
    owed[at, :] = owed[at, :] + deferred[...]


def pick_kernel(nz, leaves, levels, meta, *refs):
    lists, refs = refs[: len(levels)], refs[len(levels) :]
    own, other, picks, full = refs[:nz], refs[nz : 2 * nz], refs[2 * nz : 2 * nz + leaves], refs[2 * nz + leaves]
    height = BLOCK // leaves
    last = full.shape[0] // height - 1
    spread_parts(meta, full, own, other)
    for d in range(leaves):
        at = 0
        for (held, group), rows in zip(levels, lists):
            first = jnp.bitwise_xor(meta[2], d) * held // group
            for h in range(held):
                for k in range(rows.shape[1]):
                    block = jnp.minimum(rows[first + h, k], last)
                    picks[d][at : at + height, :] = full[pl.ds(pl.multiple_of(block * height, 8), height), :]
                    at += height


def backward_panel_kernel(nz, leaves, top, skip, before_count, meta, rows, *refs):
    picks, refs = refs[:leaves], refs[leaves:]
    own, other, refs = refs[:nz], refs[nz : 2 * nz], refs[2 * nz :]
    before, refs = refs[:before_count], refs[before_count:]
    panel, keep, send, *chain, chosen, factor, full = refs
    held, listed = rows.shape
    height = BLOCK // leaves
    part = panel.shape[0] // held
    tile = tile_of(part)
    if chain:
        chain = chain[0]
        offset = 0
        if before:
            offset = before[0].shape[0]
            chain[:offset, :] = before[0][...]
        spread_parts(meta, chain, own, other, offset)
    for h in range(held):
        for k in range(listed):
            for d in range(leaves):
                at = pl.ds(pl.multiple_of(k * BLOCK + jnp.bitwise_xor(meta[2], d) * height, 8), height)
                line = skip + (h * listed + k) * height
                chosen[at, :] = picks[d][line : line + height, :]
            if own:

                @pl.when(rows[h, k] >= top)
                def _(h=h, k=k):
                    place = pl.ds(pl.multiple_of((rows[h, k] - top) * BLOCK, BLOCK), BLOCK)
                    chosen[k * BLOCK : (k + 1) * BLOCK, :] = chain[place, :]

        for k in range(listed):
            factor[k * BLOCK : (k + 1) * BLOCK, :] = wide(chosen[k * BLOCK : (k + 1) * BLOCK, :])
        for start in range(h * part, (h + 1) * part, tile):
            full[start : start + tile, :] = times(panel[start : start + tile, :], factor[...])
    split_cores(meta, full, 0, keep, send)


def backward_sum(inv, full, h, held):
    part = inv.shape[1] // held
    tile = tile_of(part)
    total = None
    for start in range(h * part, (h + 1) * part, tile):
        term = times(inv[:, start : start + tile], wide(full[start : start + tile, :]))
        total = term if total is None else total + term
    return total


def backward_inv_kernel(nz, meta, *refs):
    own, other, (inv, solved, full) = refs[:nz], refs[nz : 2 * nz], refs[2 * nz :]
    spread_parts(meta, full, own, other)
    for h in range(solved.shape[0]):
        solved[h] = backward_sum(inv, full, h, solved.shape[0])


def backward_top_kernel(nz, leaves, meta, *refs):
    own, other, refs = refs[:nz], refs[nz : 2 * nz], refs[2 * nz :]
    inv, pieces, (full, solved) = refs[0], refs[1:-2], refs[-2:]
    spread_parts(meta, full, own, other)
    solved[...] = backward_sum(inv, full, 0, 1)
    height = BLOCK // leaves
    for d in range(leaves):
        place = jnp.bitwise_xor(meta[2], d) * height
        for b in range(solved.shape[0] // BLOCK):
            at = pl.ds(pl.multiple_of(b * BLOCK + place, 8), height)
            pieces[d][b * height : (b + 1) * height, :] = solved[at, :]


def call(kernel, name, out_shapes, scratch, flops, smem_count, *operands):
    single = not isinstance(out_shapes, (list, tuple))
    outs = [out_shapes] if single else list(out_shapes)
    moved = sum(item.size * 4 for item in operands) + sum(item.size * 4 for item in outs)
    result = pl.pallas_call(
        kernel,
        out_shape=outs,
        in_specs=[SMEM] * smem_count + [VMEM] * (len(operands) - smem_count),
        out_specs=[VMEM] * len(outs),
        scratch_shapes=scratch,
        compiler_params=pltpu.CompilerParams(vmem_limit_bytes=LIMIT),
        cost_estimate=pl.CostEstimate(flops=flops, bytes_accessed=moved, transcendentals=0),
        name=name,
    )(*operands)
    return result[0] if single else result


def shaped(*dims):
    return jax.ShapeDtypeStruct(dims, F32)


def body(*arguments):
    rhs, inv = arguments[0:4], arguments[4:8]
    panel, index_rows = (None,) + arguments[8:11], (None,) + arguments[11:14]
    leaves, devices = lax.axis_size("leaf"), lax.axis_size("rows")
    leaf, device = lax.axis_index("leaf"), lax.axis_index("rows")
    nz = devices // 2
    z, core = device // 2, device % 2
    meta = jnp.stack([z, core, leaf]).astype(jnp.int32)
    width = rhs[0].shape[2]
    counts = [item.shape[0] for item in rhs]
    owned = [item.shape[1] for item in rhs]
    sizes = [item * devices for item in owned]
    spans = [item.shape[1] for item in inv]
    helds = [max(1, spans[l] // sizes[l]) for l in range(4)]
    groups = [max(1, sizes[l] // spans[l]) for l in range(4)]
    chunks = [item // devices for item in spans]
    offsets = [sum(sizes[:l]) for l in range(5)]
    listed = [0] + [item.shape[1] // BLOCK for item in panel[1:]]

    def to_core(x):
        return lax.ppermute(x, "rows", [(r, r ^ 1) for r in range(devices)])

    def to_chip(x, k):
        return lax.ppermute(x, "rows", [(r, r ^ (2 * k)) for r in range(devices)])

    def to_leaf(x, k):
        return x if k == 0 else lax.ppermute(x, "leaf", [(i, i ^ k) for i in range(leaves)])

    def to_leaves(pieces):
        far_first = {d: to_leaf(pieces[d], d) for d in reversed(range(len(pieces)))}
        return [far_first[d] for d in range(len(pieces))]

    def scatter_chips(chunk):
        return [to_chip(chunk(k), k) for k in range(nz - 1, 0, -1)] + [chunk(0)]

    def scatter_sum(keep, send):
        received = to_core(send)
        return scatter_chips(
            lambda k: lax.dynamic_index_in_dim(keep, z ^ k, 0, False)
            + lax.dynamic_index_in_dim(received, z ^ k, 0, False)
        )

    def gather(x):
        far_first = {k: to_chip(x, k) for k in range(nz - 1, 0, -1)}
        own = [x] + [far_first[k] for k in range(1, nz)]
        return own + [to_core(item) for item in own]

    def leaf_sum(x, group):
        step = 1
        while step < group:
            x = x + to_leaf(x, step)
            step = step * 2
        return x

    def leaf_rows(x, l):
        return lax.dynamic_slice_in_dim(x, leaf * helds[l] // groups[l], helds[l], 0)

    def place(x, l):
        group, held = groups[l], helds[l]
        if leaves == group:
            return x
        out = jnp.zeros(rhs[l].shape, F32)
        for k in range(leaves // group):
            out = lax.dynamic_update_slice_in_dim(out, to_leaf(x, k * group), (leaf // group ^ k) * held, 0)
        return out

    def halves(rows):
        return [shaped(nz, rows, width), shaped(nz, rows, width)]

    def room(*dims):
        return pltpu.VMEM(dims, F32)

    solved = [None] * 4
    chain, owed = [], []
    for l in (3, 2, 1):
        keep, send = call(
            functools.partial(forward_inv_kernel, len(owed)),
            f"forward_inv_{l}",
            halves(chunks[l]),
            [room(spans[l], width)],
            6 * inv[l].size * width,
            1,
            meta,
            leaf_rows(rhs[l], l),
            *owed,
            inv[l],
        )
        solved[l] = sum(scatter_sum(keep, send)[::-1])
        parts = gather(solved[l])
        if l == 1:
            break
        keep, send, *chain = call(
            functools.partial(forward_panel_kernel, nz, len(chain), offsets[l - 1]),
            f"forward_panel_{l}",
            halves(owned[l - 1]) + ([shaped(offsets[l - 1], width)] if l > 2 else halves(owned[0])),
            [room(offsets[l], width), room(spans[l], width)],
            6 * panel[l].size * width,
            2,
            meta,
            leaf_rows(index_rows[l], l),
            *parts,
            *chain,
            panel[l],
        )
        owed = scatter_sum(keep, send)
        if groups[l - 1] > 1:
            owed = [leaf_sum(sum(owed[::-1]), groups[l - 1])]

    group, seps = groups[1], leaves // groups[1]
    height = BLOCK // group
    blocks = owned[0] // BLOCK
    deferred_keep, deferred_send = chain
    deferred_received = to_core(deferred_send)

    def leaf_cut(x, i):
        x = x.reshape(nz, seps, blocks // seps, group, height, width)
        x = lax.dynamic_slice(x, (0, i // group, 0, i % group, 0, 0), (nz, 1, blocks // seps, 1, height, width))
        return x.reshape(nz, blocks // seps * height, width)

    deferred = to_leaves([leaf_cut(deferred_keep, leaf ^ d) + leaf_cut(deferred_received, leaf ^ d) for d in range(leaves)])
    deferred = sum(deferred)
    deferred = sum(scatter_chips(lambda k: lax.dynamic_index_in_dim(deferred, z ^ k, 0, False))[::-1])

    pieces = call(
        functools.partial(forward_last_kernel, nz, group),
        "forward_panel_1",
        [shaped(listed[1] * height + 8, width)] * group,
        [room(spans[1], width), room(panel[1].shape[1], width)],
        6 * panel[1].size * width,
        2,
        meta,
        leaf_rows(index_rows[1], 1),
        *parts,
        panel[1],
    )
    piece = sum(to_leaves(pieces))
    owed = call(
        functools.partial(owed_top_kernel, nz, group, listed[1]),
        "owed_top",
        shaped(blocks * height, width),
        [],
        0,
        1,
        meta,
        *gather(piece),
        deferred,
    )
    keep, send = call(
        functools.partial(forward_top_kernel, leaves, group),
        "forward_inv_0",
        halves(chunks[0]),
        [room(owned[0], width), room(spans[0], width)],
        6 * inv[0].size * width,
        1,
        meta,
        rhs[0],
        *to_leaves([owed] * leaves),
        inv[0],
    )
    solved[0] = sum(scatter_sum(keep, send)[::-1])

    pieces = call(
        functools.partial(backward_top_kernel, nz, leaves),
        "backward_inv_0",
        [shaped(owned[0] // leaves, width)] * leaves,
        [room(spans[0], width), room(owned[0], width)],
        6 * inv[0].size * width,
        1,
        meta,
        *gather(solved[0]),
        inv[0],
    )
    piece = sum(to_leaves(pieces))
    cuts = gather(piece)
    thin = BLOCK // leaves
    top = jnp.zeros((blocks, leaves, thin, width), F32)
    for d, item in enumerate(to_leaves([piece] * leaves)):
        top = lax.dynamic_update_slice(top, item.reshape(blocks, 1, thin, width), (0, leaf ^ d, 0, 0))
    results = [top.reshape(rhs[0].shape)]

    def picked(levels, name):
        picks = call(
            functools.partial(pick_kernel, nz, leaves, [(helds[l], groups[l]) for l in levels]),
            name,
            [shaped(sum(helds[l] * listed[l] for l in levels) * thin, width)] * leaves,
            [room(sizes[0] // leaves, width)],
            0,
            1 + len(levels),
            meta,
            *[index_rows[l] for l in levels],
            *cuts,
        )
        return to_leaves(picks)

    first_picks = picked([1], "pick_1")
    later_picks = picked([2, 3], "pick_2_3")
    chain, parts = [], []
    for l in (1, 2, 3):
        above = sum(sizes[1:l])
        keep, send, *chain = call(
            functools.partial(
                backward_panel_kernel,
                nz if l > 1 else 0,
                leaves,
                sizes[0] // BLOCK,
                helds[2] * listed[2] * thin if l == 3 else 0,
                len(chain),
            ),
            f"backward_panel_{l}",
            halves(chunks[l]) + ([shaped(above, width)] if l > 1 else []),
            [
                room(panel[l].shape[1], width),
                pltpu.VMEM((panel[l].shape[1], 2 * width), BF16),
                room(spans[l], width),
            ],
            6 * panel[l].size * width,
            2,
            meta,
            leaf_rows(index_rows[l], l),
            *(first_picks if l == 1 else later_picks),
            *parts,
            *chain,
            panel[l],
        )
        residue = solved[l] - sum(scatter_sum(keep, send)[::-1])
        x = call(
            functools.partial(backward_inv_kernel, nz),
            f"backward_inv_{l}",
            shaped(helds[l], owned[l], width),
            [room(spans[l], width)],
            6 * inv[l].size * width,
            1,
            meta,
            *gather(residue),
            inv[l],
        )
        x = leaf_sum(x, groups[l])
        if l < 3:
            parts = gather(x[0])
        results.append(place(x, l))
    return tuple(results)


def solution(mesh):
    across = P(None, "rows", None)
    return jax.shard_map(
        body,
        mesh=mesh,
        in_specs=(across,) * 4 + (P("rows", "leaf"),) * 4 + (P("leaf", "rows"),) * 3 + (P(None, "rows"),) * 3,
        out_specs=(across,) * 4,
        check_vma=False,
    )
```

```python
import functools

import jax
import jax.numpy as jnp
from jax import lax
from jax.experimental import pallas as pl
from jax.experimental.pallas import tpu as pltpu
from jax.sharding import PartitionSpec as P

BLOCK = 128
F32 = jnp.float32
BF16 = jnp.bfloat16
VMEM = pl.BlockSpec(memory_space=pltpu.VMEM)
SMEM = pl.BlockSpec(memory_space=pltpu.SMEM)
LIMIT = 14 * 1024 * 1024


def cut(x):
    high = x.astype(BF16)
    return high, (x - high.astype(F32)).astype(BF16)


def wide(x):
    return jnp.concatenate(cut(x), axis=1)


def product(dims, a, xw):
    n = xw.shape[1] // 2
    high, low = cut(a)
    first = lax.dot_general(high, xw, (dims, ((), ())), preferred_element_type=F32)
    second = lax.dot_general(low, xw[:, :n], (dims, ((), ())), preferred_element_type=F32)
    return first[:, :n] + (first[:, n:] + second)


times = functools.partial(product, ((1,), (0,)))
transposed_times = functools.partial(product, ((0,), (0,)))


def tile_of(rows, largest=512):
    return min(rows, largest)


def spread_parts(meta, full, parts, offset=0):
    half = len(parts) // 2
    for k, part in enumerate(parts):
        core = meta[1] if k < half else 1 - meta[1]
        rows = part.shape[0]
        at = offset + (2 * jnp.bitwise_xor(meta[0], k % half) + core) * rows
        full[pl.ds(pl.multiple_of(at, 8), rows), :] = part[...]


def split_cores(meta, full, offset, keep, send):
    count, rows = keep.shape[0], keep.shape[1]
    for k in range(count):
        keep[k] = full[pl.ds(pl.multiple_of(offset + (2 * k + meta[1]) * rows, 8), rows), :]
        send[k] = full[pl.ds(pl.multiple_of(offset + (2 * k + 1 - meta[1]) * rows, 8), rows), :]


def forward_inv_kernel(owed_count, meta, rhs, *refs):
    owed, inv, halves, full = refs[:owed_count], refs[owed_count], refs[owed_count + 1 : -1], refs[-1]
    held = rhs.shape[0]
    part = inv.shape[1] // held
    tile = tile_of(part)
    for h in range(held):
        source = rhs[h]
        for item in owed:
            source = source - item[...]
        source = wide(source)
        for start in range(h * part, (h + 1) * part, tile):
            full[start : start + tile, :] = transposed_times(inv[:, start : start + tile], source)
    split_cores(meta, full, 0, *halves)


def forward_top_kernel(leaves, group, meta, rhs, *refs):
    owed, (inv, keep, send, source, full) = refs[:leaves], refs[leaves:]
    rows = BLOCK // group
    source[...] = rhs[0]
    for d in range(leaves):
        place = lax.rem(jnp.bitwise_xor(meta[2], d), group) * rows
        for b in range(rhs.shape[1] // BLOCK):
            at = pl.ds(pl.multiple_of(b * BLOCK + place, 8), rows)
            source[at, :] = source[at, :] - owed[d][b * rows : (b + 1) * rows, :]
    factor = wide(source[...])
    tile = tile_of(inv.shape[1])
    for start in range(0, inv.shape[1], tile):
        full[start : start + tile, :] = transposed_times(inv[:, start : start + tile], factor)
    split_cores(meta, full, 0, keep, send)


def panel_update(panel, full, h, held):
    part = panel.shape[0] // held
    tile = tile_of(part)
    update = None
    for start in range(h * part, (h + 1) * part, tile):
        term = transposed_times(panel[start : start + tile, :], wide(full[start : start + tile, :]))
        update = term if update is None else update + term
    return update


def add_blocks(chain, rows, updates, first):
    for k in range(rows.shape[0]):

        @pl.when(jnp.logical_and(rows[k] >= first, rows[k] < first + chain.shape[0] // BLOCK))
        def _(k=k):
            place = pl.ds(pl.multiple_of((rows[k] - first) * BLOCK, BLOCK), BLOCK)
            chain[place, :] = chain[place, :] + updates[k * BLOCK : (k + 1) * BLOCK, :]


def forward_panel_kernel(count, held, first, below_count, meta, rows, *refs):
    below_rows, refs = refs[:below_count], refs[below_count:]
    parts, refs = refs[:count], refs[count:]
    below, refs = refs[:below_count], refs[below_count:]
    panel, keep, send, updates, chain, full = refs
    size = updates.shape[0] // held
    spread_parts(meta, full, parts)
    for h in range(held):
        updates[h * size : (h + 1) * size, :] = panel_update(panel, full, h, held)
    chain[...] = jnp.zeros_like(chain)
    add_blocks(chain, rows, updates, first)
    for lower_rows, lower in zip(below_rows, below):
        add_blocks(chain, lower_rows, lower, first)
    split_cores(meta, chain, 0, keep, send)


def deferred_kernel(meta, upper_rows, lower_rows, upper, lower, keep, send, chain):
    chain[...] = jnp.zeros_like(chain)
    add_blocks(chain, upper_rows, upper, 0)
    add_blocks(chain, lower_rows, lower, 0)
    split_cores(meta, chain, 0, keep, send)


def leaf_cuts_kernel(group, meta, keep, received, *cuts):
    count = keep.shape[1] // BLOCK * group // len(cuts)
    height = BLOCK // group
    for d, cut in enumerate(cuts):
        other = jnp.bitwise_xor(meta[2], d)
        for b in range(count):
            row = ((other // group) * count + b) * BLOCK + lax.rem(other, group) * height
            at = pl.ds(pl.multiple_of(row, 8), height)
            for k in range(keep.shape[0]):
                cut[k, b * height : (b + 1) * height, :] = keep[k, at, :] + received[k, at, :]


def forward_last_kernel(count, group, meta, rows, *refs):
    parts, refs = refs[:count], refs[count:]
    panel, pieces, (full, update) = refs[0], refs[1:-2], refs[-2:]
    spread_parts(meta, full, parts)
    update[...] = panel_update(panel, full, 0, 1)
    listed = rows.shape[0]
    height = BLOCK // group
    for d in range(group):
        place = jnp.bitwise_xor(lax.rem(meta[2], group), d) * height
        for k in range(listed):
            at = pl.ds(pl.multiple_of(k * BLOCK + place, 8), height)
            pieces[d][k * height : (k + 1) * height, :] = update[at, :]
        tail = pieces[d].shape[0] - listed * height
        numbers = jnp.zeros((tail, update.shape[1]), F32)
        if d == 0:
            line = lax.broadcasted_iota(jnp.int32, numbers.shape, 0)
            for k in range(listed):
                numbers = jnp.where(line == k, rows[k].astype(F32), numbers)
        pieces[d][listed * height :, :] = numbers


def owed_top_kernel(nz, group, listed, meta, *refs):
    parts, owed = refs[:-1], refs[-1]
    height = BLOCK // group
    blocks = owed.shape[0] // height
    first = (2 * meta[0] + meta[1]) * blocks
    for b in range(blocks):
        wanted = (first + b).astype(F32)
        total = jnp.zeros((height, owed.shape[1]), F32)
        for item in parts:
            for k in range(listed):
                number = item[listed * height + k : listed * height + k + 1, :]
                total = total + jnp.where(number == wanted, item[k * height : (k + 1) * height, :], 0.0)
        owed[b * height : (b + 1) * height, :] = total
    start = parts[nz].shape[0]
    count = parts[0].shape[0] - start
    at = pl.ds(pl.multiple_of((meta[2] // group) * count, 8), count)
    total = owed[at, :]
    for item in parts[:nz]:
        total = total + item[start:, :]
    owed[at, :] = total


def pick_kernel(count, leaves, levels, meta, *refs):
    lists, refs = refs[: len(levels)], refs[len(levels) :]
    parts, picks, full = refs[:count], refs[count:-1], refs[-1]
    height = BLOCK // leaves
    last = full.shape[0] // height - 1
    spread_parts(meta, full, parts)
    for d in range(leaves):
        at = 0
        for (held, group, listed), rows in zip(levels, lists):
            first = jnp.bitwise_xor(meta[2], d) * held // group
            for h in range(held):
                for k in range(listed):
                    block = jnp.minimum(rows[(first + h) * listed + k], last)
                    picks[d][at : at + height, :] = full[pl.ds(pl.multiple_of(block * height, 8), height), :]
                    at += height


def backward_panel_kernel(count, leaves, held, top, skip, before_count, meta, rows, *refs):
    picks, refs = refs[:leaves], refs[leaves:]
    parts, refs = refs[:count], refs[count:]
    before, refs = refs[:before_count], refs[before_count:]
    panel, halves, chain, (chosen, factor, full) = refs[0], refs[1:3], refs[3:-3], refs[-3:]
    listed = rows.shape[0] // held
    height = BLOCK // leaves
    part = panel.shape[0] // held
    tile = tile_of(part)
    if chain:
        chain = chain[0]
        offset = 0
        if before:
            offset = before[0].shape[0]
            chain[:offset, :] = before[0][...]
        spread_parts(meta, chain, parts, offset)
    for h in range(held):
        for k in range(listed):
            for d in range(leaves):
                at = pl.ds(pl.multiple_of(k * BLOCK + jnp.bitwise_xor(meta[2], d) * height, 8), height)
                line = skip + (h * listed + k) * height
                chosen[at, :] = picks[d][line : line + height, :]
            if parts:

                @pl.when(rows[h * listed + k] >= top)
                def _(h=h, k=k):
                    place = pl.ds(pl.multiple_of((rows[h * listed + k] - top) * BLOCK, BLOCK), BLOCK)
                    chosen[k * BLOCK : (k + 1) * BLOCK, :] = chain[place, :]

        for k in range(listed):
            factor[k * BLOCK : (k + 1) * BLOCK, :] = wide(chosen[k * BLOCK : (k + 1) * BLOCK, :])
        for start in range(h * part, (h + 1) * part, tile):
            full[start : start + tile, :] = times(panel[start : start + tile, :], factor[...])
    split_cores(meta, full, 0, *halves)


def backward_sum(inv, full, h, held):
    part = inv.shape[1] // held
    tile = tile_of(part)
    total = None
    for start in range(h * part, (h + 1) * part, tile):
        term = times(inv[:, start : start + tile], wide(full[start : start + tile, :]))
        total = term if total is None else total + term
    return total


def backward_inv_kernel(meta, *refs):
    parts, (inv, solved, full) = refs[:-3], refs[-3:]
    spread_parts(meta, full, parts)
    for h in range(solved.shape[0]):
        solved[h] = backward_sum(inv, full, h, solved.shape[0])


def backward_top_kernel(count, leaves, meta, *refs):
    parts, refs = refs[:count], refs[count:]
    inv, pieces, (full, solved) = refs[0], refs[1:-2], refs[-2:]
    spread_parts(meta, full, parts)
    solved[...] = backward_sum(inv, full, 0, 1)
    height = BLOCK // leaves
    for d in range(leaves):
        place = jnp.bitwise_xor(meta[2], d) * height
        for b in range(solved.shape[0] // BLOCK):
            at = pl.ds(pl.multiple_of(b * BLOCK + place, 8), height)
            pieces[d][b * height : (b + 1) * height, :] = solved[at, :]


def call(kernel, name, out_shapes, scratch, flops, smem_count, *operands):
    single = not isinstance(out_shapes, (list, tuple))
    outs = [out_shapes] if single else list(out_shapes)
    moved = sum(item.size * 4 for item in operands) + sum(item.size * 4 for item in outs)
    result = pl.pallas_call(
        kernel,
        out_shape=outs,
        in_specs=[SMEM] * smem_count + [VMEM] * (len(operands) - smem_count),
        out_specs=[VMEM] * len(outs),
        scratch_shapes=scratch,
        compiler_params=pltpu.CompilerParams(vmem_limit_bytes=LIMIT),
        cost_estimate=pl.CostEstimate(flops=flops, bytes_accessed=moved, transcendentals=0),
        name=name,
    )(*operands)
    return result[0] if single else result


def spacer_kernel(x, dependency, out):
    out[...] = x[...]


BESIDE = 40_000_000_000


def beside(x, dependency):
    return pl.pallas_call(
        spacer_kernel,
        out_shape=jax.ShapeDtypeStruct(x.shape, x.dtype),
        in_specs=[VMEM, pl.BlockSpec(memory_space=pl.ANY)],
        out_specs=VMEM,
        compiler_params=pltpu.CompilerParams(vmem_limit_bytes=1024 * 1024),
        cost_estimate=pl.CostEstimate(flops=BESIDE, bytes_accessed=2 * x.size * 4, transcendentals=0),
        name="beside",
    )(x, dependency)


def shaped(*dims):
    return jax.ShapeDtypeStruct(dims, F32)


def after(x, *others):
    return lax.optimization_barrier((x, others))[0]


def body(*arguments):
    rhs, inv = arguments[0:4], arguments[4:8]
    panel, index_rows = (None,) + arguments[8:11], (None,) + arguments[11:14]
    leaves, devices = lax.axis_size("leaf"), lax.axis_size("rows")
    leaf, device = lax.axis_index("leaf"), lax.axis_index("rows")
    nz = devices // 2
    z, core = device // 2, device % 2
    meta = jnp.stack([z, core, leaf]).astype(jnp.int32)
    width = rhs[0].shape[2]
    owned = [item.shape[1] for item in rhs]
    sizes = [item * devices for item in owned]
    spans = [item.shape[1] for item in inv]
    helds = [max(1, spans[l] // sizes[l]) for l in range(4)]
    groups = [max(1, sizes[l] // spans[l]) for l in range(4)]
    chunks = [item // devices for item in spans]
    listed = [0] + [item.shape[1] // BLOCK for item in panel[1:]]

    def to_core(x):
        return lax.ppermute(x, "rows", [(r, r ^ 1) for r in range(devices)])

    def to_chip(x, k):
        return lax.ppermute(x, "rows", [(r, r ^ (2 * k)) for r in range(devices)])

    def to_leaf(x, k):
        return x if k == 0 else lax.ppermute(x, "leaf", [(i, i ^ k) for i in range(leaves)])

    def to_leaves(pieces):
        far_first = {d: to_leaf(pieces[d], d) for d in reversed(range(len(pieces)))}
        return [far_first[d] for d in range(len(pieces))]

    def scatter_chips(chunk):
        far_first = {k: to_chip(chunk(k), k) for k in range(nz - 1, 0, -1)}
        return [chunk(0)] + [far_first[k] for k in range(1, nz)]

    def scatter_parts(keep, send):
        received = to_core(send)
        return scatter_chips(
            lambda k: lax.dynamic_index_in_dim(keep, z ^ k, 0, False)
            + lax.dynamic_index_in_dim(received, z ^ k, 0, False)
        )

    def scatter_sum(keep, send):
        return sum(scatter_parts(keep, send))

    def gather(x):
        far_first = {k: to_chip(x, k) for k in range(nz - 1, 0, -1)}
        own = [x] + [far_first[k] for k in range(1, nz)]
        return own + [to_core(item) for item in own]

    def leaf_sum(x, group):
        step = 1
        while step < group:
            x = x + to_leaf(x, step)
            step = step * 2
        return x

    def leaf_rows(x, l):
        return lax.dynamic_slice_in_dim(x, leaf * helds[l] // groups[l], helds[l], 0)

    def flat_rows(l, first, count):
        width_rows = index_rows[l].shape[1]
        at = lax.iota(jnp.int32, count * width_rows)[:, None, None]
        seps = lax.broadcasted_iota(jnp.int32, (1,) + index_rows[l].shape, 1)
        line = lax.broadcasted_iota(jnp.int32, (1,) + index_rows[l].shape, 2)
        wanted = (seps - first) * width_rows + line == at
        return jnp.sum(jnp.where(wanted, index_rows[l][None], 0), axis=(1, 2))

    all_rows = [None] + [flat_rows(l, 0, index_rows[l].shape[0]) for l in (1, 2, 3)]
    own_rows = [None] + [flat_rows(l, leaf * helds[l] // groups[l], helds[l]) for l in (1, 2, 3)]

    def other_groups(x, l):
        return [x] + [to_leaf(x, k * groups[l]) for k in range(1, leaves // groups[l])]

    def place(parts, l):
        out = jnp.zeros(rhs[l].shape, F32)
        for k, item in enumerate(parts):
            out = lax.dynamic_update_slice_in_dim(out, item, (leaf // groups[l] ^ k) * helds[l], 0)
        return out

    def halves(rows):
        return [shaped(nz, rows, width)] * 2

    def room(*dims):
        return pltpu.VMEM(dims, F32)

    def forward_inv(l, owed):
        return call(
            functools.partial(forward_inv_kernel, len(owed)),
            f"forward_inv_{l}",
            halves(chunks[l]),
            [room(spans[l], width)],
            6 * inv[l].size * width,
            1,
            meta,
            leaf_rows(rhs[l], l),
            *owed,
            inv[l],
        )

    solved = [None] * 4

    solved[3] = scatter_sum(*forward_inv(3, []))
    def forward_panel(l, below):
        parts = gather(solved[l])
        return call(
            functools.partial(forward_panel_kernel, len(parts), helds[l], sum(sizes[: l - 1]) // BLOCK, len(below)),
            f"forward_panel_{l}",
            halves(owned[l - 1]) + [shaped(helds[l] * listed[l] * BLOCK, width)],
            [room(sizes[l - 1], width), room(spans[l], width)],
            6 * panel[l].size * width,
            2 + len(below),
            meta,
            own_rows[l],
            *[own_rows[item] for item in below],
            *parts,
            *[updates[item] for item in below],
            panel[l],
        )

    updates = [None] * 4
    keep, send, updates[3] = forward_panel(3, [])

    def owed_parts(parts, l):
        return parts if groups[l] == 1 else [leaf_sum(sum(parts), groups[l])]

    solved[2] = scatter_sum(*forward_inv(2, owed_parts(scatter_parts(keep, send), 2)))
    keep, send, updates[2] = forward_panel(2, [3])
    parts = scatter_parts(keep, send)

    group, seps = groups[1], leaves // groups[1]
    height = BLOCK // group
    blocks = owned[0] // BLOCK
    parts = scatter_parts(*forward_inv(1, owed_parts(parts, 1)))
    top_keep, top_send = call(
        deferred_kernel,
        "deferred",
        halves(owned[0]),
        [room(sizes[0], width)],
        BESIDE,
        3,
        meta,
        own_rows[2],
        own_rows[3],
        after(updates[2], parts[0]),
        updates[3],
    )
    leaf_cuts = call(
        functools.partial(leaf_cuts_kernel, group),
        "leaf_cuts",
        [shaped(nz, owned[0] // leaves, width)] * leaves,
        [],
        0,
        1,
        meta,
        top_keep,
        to_core(top_send),
    )
    parts, leaf_cuts = lax.optimization_barrier((parts, leaf_cuts))
    deferred = to_leaves(leaf_cuts)
    solved[1] = sum(parts)

    parts = gather(solved[1])
    pieces = call(
        functools.partial(forward_last_kernel, len(parts), group),
        "forward_panel_1",
        [shaped(listed[1] * height + 8, width)] * group,
        [room(spans[1], width), room(panel[1].shape[1], width)],
        6 * panel[1].size * width,
        2,
        meta,
        own_rows[1],
        *parts,
        panel[1],
    )
    piece, deferred = sum(to_leaves(pieces)), sum(deferred)
    own = scatter_chips(
        lambda k: jnp.concatenate([piece, lax.dynamic_index_in_dim(deferred, z ^ k, 0, False)], axis=0)
    )
    owed = call(
        functools.partial(owed_top_kernel, nz, group, listed[1]),
        "owed_top",
        shaped(blocks * height, width),
        [],
        0,
        1,
        meta,
        *own,
        *[to_core(item[: piece.shape[0]]) for item in own],
    )
    keep, send = call(
        functools.partial(forward_top_kernel, leaves, group),
        "forward_inv_0",
        halves(chunks[0]),
        [room(owned[0], width), room(spans[0], width)],
        6 * inv[0].size * width,
        1,
        meta,
        rhs[0],
        *to_leaves([owed] * leaves),
        inv[0],
    )
    solved[0] = scatter_sum(keep, send)

    parts = gather(solved[0])
    pieces = call(
        functools.partial(backward_top_kernel, len(parts), leaves),
        "backward_inv_0",
        [shaped(owned[0] // leaves, width)] * leaves,
        [room(spans[0], width), room(owned[0], width)],
        6 * inv[0].size * width,
        1,
        meta,
        *parts,
        inv[0],
    )
    piece = sum(to_leaves(pieces))
    quarters = gather(piece)
    top_parts = to_leaves([beside(piece, piece)] * leaves)

    def picked(levels, name, quarters, cost):
        picks = call(
            functools.partial(pick_kernel, len(quarters), leaves, [(helds[l], groups[l], listed[l]) for l in levels]),
            name,
            [shaped(sum(helds[l] * listed[l] for l in levels) * (BLOCK // leaves), width)] * leaves,
            [room(sizes[0] // leaves, width)],
            cost,
            1 + len(levels),
            meta,
            *[all_rows[l] for l in levels],
            *quarters,
        )
        return to_leaves(picks)

    thin = BLOCK // leaves
    quarters, top_parts = lax.optimization_barrier((quarters, top_parts))
    top = jnp.zeros((blocks, leaves, thin, width), F32)
    for d, item in enumerate(top_parts):
        top = lax.dynamic_update_slice(top, item.reshape(blocks, 1, thin, width), (0, leaf ^ d, 0, 0))
    results = [top.reshape(rhs[0].shape)]
    picks = picked([1], "pick_1", quarters, 0)
    chain, parts = [], []
    for l in (1, 2, 3):
        above = sum(sizes[1:l])
        keep, send, *chain = call(
            functools.partial(
                backward_panel_kernel,
                len(parts),
                leaves,
                helds[l],
                sizes[0] // BLOCK,
                helds[2] * listed[2] * thin if l == 3 else 0,
                len(chain),
            ),
            f"backward_panel_{l}",
            halves(chunks[l]) + ([shaped(above, width)] if l > 1 else []),
            [
                room(panel[l].shape[1], width),
                pltpu.VMEM((panel[l].shape[1], 2 * width), BF16),
                room(spans[l], width),
            ],
            6 * panel[l].size * width,
            2,
            meta,
            own_rows[l],
            *picks,
            *parts,
            *chain,
            panel[l],
        )
        residue = solved[l] - scatter_sum(keep, send)
        if l == 1:
            picks = picked([2, 3], "pick_2_3", after(quarters, residue), BESIDE)
        x = call(
            backward_inv_kernel,
            f"backward_inv_{l}",
            shaped(helds[l], owned[l], width),
            [room(spans[l], width)],
            6 * inv[l].size * width,
            1,
            meta,
            *gather(residue),
            inv[l],
        )
        if l == 1:
            x, picks = lax.optimization_barrier((x, picks))
        x = leaf_sum(x, groups[l])
        if l < 3:
            parts = gather(x[0])
            placed = [x] + other_groups(beside(x, x), l)[1:]
            parts, placed = lax.optimization_barrier((parts, placed))
            results.append(place(placed, l))
    results.append(place(other_groups(x, 3), 3))
    return tuple(results)


def solution(mesh):
    across = P(None, "rows", None)
    return jax.shard_map(
        body,
        mesh=mesh,
        in_specs=(across,) * 4 + (P("rows", "leaf"),) * 4 + (P("leaf", "rows"),) * 3 + (P(None, "rows"),) * 3,
        out_specs=(across,) * 4,
        check_vma=False,
    )
```

```python
import functools

import jax
import jax.numpy as jnp
from jax import lax
from jax.experimental import pallas as pl
from jax.experimental.pallas import tpu as pltpu
from jax.sharding import PartitionSpec as P

BLOCK = 128
F32 = jnp.float32
BF16 = jnp.bfloat16
VMEM = pl.BlockSpec(memory_space=pltpu.VMEM)
SMEM = pl.BlockSpec(memory_space=pltpu.SMEM)
LIMIT = 14 * 1024 * 1024


def cut(x):
    high = x.astype(BF16)
    return high, (x - high.astype(F32)).astype(BF16)


def wide(x):
    return jnp.concatenate(cut(x), axis=1)


def product(dims, a, xw):
    n = xw.shape[1] // 2
    high, low = cut(a)
    first = lax.dot_general(high, xw, (dims, ((), ())), preferred_element_type=F32)
    second = lax.dot_general(low, xw[:, :n], (dims, ((), ())), preferred_element_type=F32)
    return first[:, :n] + (first[:, n:] + second)


times = functools.partial(product, ((1,), (0,)))
transposed_times = functools.partial(product, ((0,), (0,)))


def tile_of(rows, largest=512):
    return min(rows, largest)


def spread_parts(meta, full, parts, offset=0):
    half = len(parts) // 2
    for k, part in enumerate(parts):
        core = meta[1] if k < half else 1 - meta[1]
        rows = part.shape[0]
        at = offset + (2 * jnp.bitwise_xor(meta[0], k % half) + core) * rows
        full[pl.ds(pl.multiple_of(at, 8), rows), :] = part[...]


def split_cores(meta, full, offset, keep, send):
    count, rows = keep.shape[0], keep.shape[1]
    for k in range(count):
        keep[k] = full[pl.ds(pl.multiple_of(offset + (2 * k + meta[1]) * rows, 8), rows), :]
        send[k] = full[pl.ds(pl.multiple_of(offset + (2 * k + 1 - meta[1]) * rows, 8), rows), :]


def forward_inv_kernel(owed_count, meta, rhs, *refs):
    owed, inv, halves, full = refs[:owed_count], refs[owed_count], refs[owed_count + 1 : -1], refs[-1]
    held = rhs.shape[0]
    part = inv.shape[1] // held
    tile = tile_of(part)
    for h in range(held):
        source = rhs[h]
        for item in owed:
            source = source - item[...]
        source = wide(source)
        for start in range(h * part, (h + 1) * part, tile):
            full[start : start + tile, :] = transposed_times(inv[:, start : start + tile], source)
    split_cores(meta, full, 0, *halves)


def forward_top_kernel(leaves, meta, rhs, *refs):
    owed, (inv, keep, send, source, full) = refs[:leaves], refs[leaves:]
    height = BLOCK // leaves
    source[...] = rhs[0]
    for d in range(leaves):
        place = jnp.bitwise_xor(meta[2], d) * height
        for b in range(rhs.shape[1] // BLOCK):
            at = pl.ds(pl.multiple_of(b * BLOCK + place, 8), height)
            source[at, :] = source[at, :] - owed[d][b * height : (b + 1) * height, :]
    factor = wide(source[...])
    tile = tile_of(inv.shape[1])
    for start in range(0, inv.shape[1], tile):
        full[start : start + tile, :] = transposed_times(inv[:, start : start + tile], factor)
    split_cores(meta, full, 0, keep, send)


def panel_update(panel, full, h, held):
    part = panel.shape[0] // held
    tile = tile_of(part)
    update = None
    for start in range(h * part, (h + 1) * part, tile):
        term = transposed_times(panel[start : start + tile, :], wide(full[start : start + tile, :]))
        update = term if update is None else update + term
    return update


def add_blocks(chain, rows, updates, first):
    for k in range(rows.shape[0]):

        @pl.when(jnp.logical_and(rows[k] >= first, rows[k] < first + chain.shape[0] // BLOCK))
        def _(k=k):
            place = pl.ds(pl.multiple_of((rows[k] - first) * BLOCK, BLOCK), BLOCK)
            chain[place, :] = chain[place, :] + updates[k * BLOCK : (k + 1) * BLOCK, :]


def forward_panel_kernel(count, held, first, below_count, meta, rows, *refs):
    below_rows, refs = refs[:below_count], refs[below_count:]
    parts, refs = refs[:count], refs[count:]
    below, refs = refs[:below_count], refs[below_count:]
    panel, keep, send, updates, chain, full = refs
    size = updates.shape[0] // held
    spread_parts(meta, full, parts)
    for h in range(held):
        updates[h * size : (h + 1) * size, :] = panel_update(panel, full, h, held)
    chain[...] = jnp.zeros_like(chain)
    add_blocks(chain, rows, updates, first)
    for lower_rows, lower in zip(below_rows, below):
        add_blocks(chain, lower_rows, lower, first)
    split_cores(meta, chain, 0, keep, send)


def deferred_kernel(meta, upper_rows, lower_rows, upper, lower, keep, send, chain):
    leaves, count, rows = keep.shape[:3]
    height = BLOCK // leaves
    blocks = rows // height
    chain[...] = jnp.zeros_like(chain)
    add_blocks(chain, upper_rows, upper, 0)
    add_blocks(chain, lower_rows, lower, 0)
    for i in range(leaves):
        for k in range(count):
            for b in range(blocks):
                line = slice(b * height, (b + 1) * height)
                own = ((2 * k + meta[1]) * blocks + b) * BLOCK + i * height
                other = ((2 * k + 1 - meta[1]) * blocks + b) * BLOCK + i * height
                keep[i, k, line, :] = chain[pl.ds(pl.multiple_of(own, 8), height), :]
                send[i, k, line, :] = chain[pl.ds(pl.multiple_of(other, 8), height), :]


def leaf_cuts_kernel(meta, keep, received, dependency, *cuts):
    for d, cut in enumerate(cuts):
        other = jnp.bitwise_xor(meta[2], d)
        cut[...] = keep[other] + received[other]


def forward_last_kernel(nz, group, leaves, meta, rows, *refs):
    parts, refs = refs[: 2 * nz], refs[2 * nz :]
    panel, pieces, (full, update) = refs[0], refs[1:-2], refs[-2:]
    spread_parts(meta, full, parts)
    update[...] = panel_update(panel, full, 0, 1)
    listed = rows.shape[0]
    height = BLOCK // leaves
    for d in range(leaves):
        place = jnp.bitwise_xor(meta[2], d) * height
        for k in range(listed):
            at = pl.ds(pl.multiple_of(k * BLOCK + place, 8), height)
            pieces[d][k * height : (k + 1) * height, :] = update[at, :]
        tail = pieces[d].shape[0] - listed * height
        numbers = jnp.zeros((tail, update.shape[1]), F32)
        if d % group == 0:
            line = lax.broadcasted_iota(jnp.int32, numbers.shape, 0)
            for k in range(listed):
                numbers = jnp.where(line == k, rows[k].astype(F32), numbers)
        pieces[d][listed * height :, :] = numbers


def owed_top_kernel(listed, height, meta, *refs):
    parts, owed = refs[:-1], refs[-1]
    blocks = owed.shape[0] // height
    start = parts[-1].shape[0]
    size = listed * height + 8
    first = (2 * meta[0] + meta[1]) * blocks
    for b in range(blocks):
        wanted = (first + b).astype(F32)
        total = jnp.zeros((height, owed.shape[1]), F32)
        for item in parts:
            if item.shape[0] > start:
                total = total + item[start + b * height : start + (b + 1) * height, :]
            for at in range(0, start, size):
                for k in range(listed):
                    number = item[at + listed * height + k : at + listed * height + k + 1, :]
                    term = item[at + k * height : at + (k + 1) * height, :]
                    total = total + jnp.where(number == wanted, term, 0.0)
        owed[b * height : (b + 1) * height, :] = total


def pick_kernel(count, leaves, levels, meta, *refs):
    lists, refs = refs[: len(levels)], refs[len(levels) :]
    parts, picks, full = refs[:count], refs[count:-1], refs[-1]
    height = BLOCK // leaves
    last = full.shape[0] // height - 1
    spread_parts(meta, full, parts)
    for d in range(leaves):
        at = 0
        for (held, group, listed), rows in zip(levels, lists):
            first = jnp.bitwise_xor(meta[2], d) * held // group
            for h in range(held):
                for k in range(listed):
                    block = jnp.minimum(rows[(first + h) * listed + k], last)
                    picks[d][at : at + height, :] = full[pl.ds(pl.multiple_of(block * height, 8), height), :]
                    at += height


def backward_panel_kernel(count, leaves, held, top, skip, before_count, meta, rows, *refs):
    picks, refs = refs[:leaves], refs[leaves:]
    parts, refs = refs[:count], refs[count:]
    before, refs = refs[:before_count], refs[before_count:]
    panel, halves, chain, (chosen, factor, full) = refs[0], refs[1:3], refs[3:-3], refs[-3:]
    listed = rows.shape[0] // held
    height = BLOCK // leaves
    part = panel.shape[0] // held
    tile = tile_of(part)
    if chain:
        chain = chain[0]
        offset = 0
        if before:
            offset = before[0].shape[0]
            chain[:offset, :] = before[0][...]
        spread_parts(meta, chain, parts, offset)
    for h in range(held):
        for k in range(listed):
            for d in range(leaves):
                at = pl.ds(pl.multiple_of(k * BLOCK + jnp.bitwise_xor(meta[2], d) * height, 8), height)
                line = skip + (h * listed + k) * height
                chosen[at, :] = picks[d][line : line + height, :]
            if parts:

                @pl.when(rows[h * listed + k] >= top)
                def _(h=h, k=k):
                    place = pl.ds(pl.multiple_of((rows[h * listed + k] - top) * BLOCK, BLOCK), BLOCK)
                    chosen[k * BLOCK : (k + 1) * BLOCK, :] = chain[place, :]

        for k in range(listed):
            factor[k * BLOCK : (k + 1) * BLOCK, :] = wide(chosen[k * BLOCK : (k + 1) * BLOCK, :])
        for start in range(h * part, (h + 1) * part, tile):
            full[start : start + tile, :] = times(panel[start : start + tile, :], factor[...])
    split_cores(meta, full, 0, *halves)


def backward_sum(inv, full, h, held):
    part = inv.shape[1] // held
    tile = tile_of(part)
    total = None
    for start in range(h * part, (h + 1) * part, tile):
        term = times(inv[:, start : start + tile], wide(full[start : start + tile, :]))
        total = term if total is None else total + term
    return total


def backward_inv_kernel(meta, *refs):
    parts, (inv, solved, full) = refs[:-3], refs[-3:]
    spread_parts(meta, full, parts)
    for h in range(solved.shape[0]):
        solved[h] = backward_sum(inv, full, h, solved.shape[0])


def backward_top_kernel(count, leaves, meta, *refs):
    parts, refs = refs[:count], refs[count:]
    inv, pieces, (full, solved) = refs[0], refs[1:-2], refs[-2:]
    spread_parts(meta, full, parts)
    solved[...] = backward_sum(inv, full, 0, 1)
    height = BLOCK // leaves
    for d in range(leaves):
        place = jnp.bitwise_xor(meta[2], d) * height
        for b in range(solved.shape[0] // BLOCK):
            at = pl.ds(pl.multiple_of(b * BLOCK + place, 8), height)
            pieces[d][b * height : (b + 1) * height, :] = solved[at, :]


def call(kernel, name, out_shapes, scratch, flops, smem_count, *operands):
    single = not isinstance(out_shapes, (list, tuple))
    outs = [out_shapes] if single else list(out_shapes)
    moved = sum(item.size * 4 for item in operands) + sum(item.size * 4 for item in outs)
    result = pl.pallas_call(
        kernel,
        out_shape=outs,
        in_specs=[SMEM] * smem_count + [VMEM] * (len(operands) - smem_count),
        out_specs=[VMEM] * len(outs),
        scratch_shapes=scratch,
        compiler_params=pltpu.CompilerParams(vmem_limit_bytes=LIMIT),
        cost_estimate=pl.CostEstimate(flops=flops, bytes_accessed=moved, transcendentals=0),
        name=name,
    )(*operands)
    return result[0] if single else result


def spacer_kernel(x, dependency, out):
    out[...] = x[...]


BESIDE = 40_000_000_000


def beside(x, dependency):
    return pl.pallas_call(
        spacer_kernel,
        out_shape=jax.ShapeDtypeStruct(x.shape, x.dtype),
        in_specs=[VMEM, pl.BlockSpec(memory_space=pl.ANY)],
        out_specs=VMEM,
        compiler_params=pltpu.CompilerParams(vmem_limit_bytes=1024 * 1024),
        cost_estimate=pl.CostEstimate(flops=BESIDE, bytes_accessed=2 * x.size * 4, transcendentals=0),
        name="beside",
    )(x, dependency)


def shaped(*dims):
    return jax.ShapeDtypeStruct(dims, F32)


def after(x, *others):
    return lax.optimization_barrier((x, others))[0]


def body(*arguments):
    rhs, inv = arguments[0:4], arguments[4:8]
    panel, index_rows = (None,) + arguments[8:11], (None,) + arguments[11:14]
    leaves, devices = lax.axis_size("leaf"), lax.axis_size("rows")
    leaf, device = lax.axis_index("leaf"), lax.axis_index("rows")
    nz = devices // 2
    z, core = device // 2, device % 2
    meta = jnp.stack([z, core, leaf]).astype(jnp.int32)
    width = rhs[0].shape[2]
    owned = [item.shape[1] for item in rhs]
    sizes = [item * devices for item in owned]
    spans = [item.shape[1] for item in inv]
    helds = [max(1, spans[l] // sizes[l]) for l in range(4)]
    groups = [max(1, sizes[l] // spans[l]) for l in range(4)]
    chunks = [item // devices for item in spans]
    listed = [0] + [item.shape[1] // BLOCK for item in panel[1:]]

    def to_core(x):
        return lax.ppermute(x, "rows", [(r, r ^ 1) for r in range(devices)])

    def to_chip(x, k):
        return lax.ppermute(x, "rows", [(r, r ^ (2 * k)) for r in range(devices)])

    def to_leaf(x, k):
        return x if k == 0 else lax.ppermute(x, "leaf", [(i, i ^ k) for i in range(leaves)])

    def to_leaves(pieces):
        far_first = {d: to_leaf(pieces[d], d) for d in reversed(range(len(pieces)))}
        return [far_first[d] for d in range(len(pieces))]

    def scatter_chips(chunk):
        far_first = {k: to_chip(chunk(k), k) for k in range(nz - 1, 0, -1)}
        return [chunk(0)] + [far_first[k] for k in range(1, nz)]

    def scatter_parts(keep, send):
        received = to_core(send)
        return scatter_chips(
            lambda k: lax.dynamic_index_in_dim(keep, z ^ k, 0, False)
            + lax.dynamic_index_in_dim(received, z ^ k, 0, False)
        )

    def scatter_sum(keep, send):
        return sum(scatter_parts(keep, send))

    def gather(x):
        far_first = {k: to_chip(x, k) for k in range(nz - 1, 0, -1)}
        own = [x] + [far_first[k] for k in range(1, nz)]
        return own + [to_core(item) for item in own]

    def leaf_sum(x, group):
        step = 1
        while step < group:
            x = x + to_leaf(x, step)
            step = step * 2
        return x

    def leaf_rows(x, l):
        return lax.dynamic_slice_in_dim(x, leaf * helds[l] // groups[l], helds[l], 0)

    def flat_rows(l, first, count):
        width_rows = index_rows[l].shape[1]
        at = lax.iota(jnp.int32, count * width_rows)[:, None, None]
        seps = lax.broadcasted_iota(jnp.int32, (1,) + index_rows[l].shape, 1)
        line = lax.broadcasted_iota(jnp.int32, (1,) + index_rows[l].shape, 2)
        wanted = (seps - first) * width_rows + line == at
        return jnp.sum(jnp.where(wanted, index_rows[l][None], 0), axis=(1, 2))

    def small_arrays():
        own = [flat_rows(l, leaf * helds[l] // groups[l], helds[l]) for l in (1, 2, 3)]
        every = [flat_rows(l, 0, index_rows[l].shape[0]) for l in (1, 2, 3)]
        return own, every, [leaf_rows(rhs[l], l) for l in (1, 2)]

    def other_groups(x, l):
        return [x] + [to_leaf(x, k * groups[l]) for k in range(1, leaves // groups[l])]

    def place(parts, l):
        out = jnp.zeros(rhs[l].shape, F32)
        for k, item in enumerate(parts):
            out = lax.dynamic_update_slice_in_dim(out, item, (leaf // groups[l] ^ k) * helds[l], 0)
        return out

    def halves(rows):
        return [shaped(nz, rows, width)] * 2

    def room(*dims):
        return pltpu.VMEM(dims, F32)

    def forward_inv(l, owed):
        return call(
            functools.partial(forward_inv_kernel, len(owed)),
            f"forward_inv_{l}",
            halves(chunks[l]),
            [room(spans[l], width)],
            6 * inv[l].size * width,
            1,
            meta,
            own_rhs[l],
            *owed,
            inv[l],
        )

    solved = [None] * 4

    own_rhs = [None, None, None, leaf_rows(rhs[3], 3)]
    parts = scatter_parts(*forward_inv(3, []))
    index_rows = (None,) + after(arguments[11:14], parts[0])
    parts, (own_rows, all_rows, early) = lax.optimization_barrier((parts, small_arrays()))
    own_rows, all_rows, own_rhs = [None] + own_rows, [None] + all_rows, [None] + early + own_rhs[3:]
    solved[3] = sum(parts)
    def forward_panel(l, below):
        parts = gather(solved[l])
        return call(
            functools.partial(forward_panel_kernel, len(parts), helds[l], sum(sizes[: l - 1]) // BLOCK, len(below)),
            f"forward_panel_{l}",
            halves(owned[l - 1]) + [shaped(helds[l] * listed[l] * BLOCK, width)],
            [room(sizes[l - 1], width), room(spans[l], width)],
            6 * panel[l].size * width,
            2 + len(below),
            meta,
            own_rows[l],
            *[own_rows[item] for item in below],
            *parts,
            *[updates[item] for item in below],
            panel[l],
        )

    updates = [None] * 4
    keep, send, updates[3] = forward_panel(3, [])

    def owed_parts(parts, l):
        if groups[l] == 1:
            return parts
        total = sum(parts)
        return [total, to_leaf(total, 1)] if groups[l] == 2 else [leaf_sum(total, groups[l])]

    solved[2] = scatter_sum(*forward_inv(2, owed_parts(scatter_parts(keep, send), 2)))
    keep, send, updates[2] = forward_panel(2, [3])
    parts = scatter_parts(keep, send)

    group, thin = groups[1], BLOCK // leaves
    top_rows = owned[0] // leaves
    top_keep, top_send = call(
        deferred_kernel,
        "deferred",
        [shaped(leaves, nz, top_rows, width)] * 2,
        [room(sizes[0], width)],
        0,
        3,
        meta,
        own_rows[2],
        own_rows[3],
        updates[2],
        updates[3],
    )
    leaf_cuts = call(
        leaf_cuts_kernel,
        "leaf_cuts",
        [shaped(nz, top_rows, width)] * leaves,
        [],
        BESIDE,
        1,
        meta,
        top_keep,
        to_core(top_send),
        parts[0],
    )
    deferred = to_leaves(leaf_cuts)
    solved[1] = scatter_sum(*forward_inv(1, owed_parts(parts, 1)))

    pieces = call(
        functools.partial(forward_last_kernel, nz, group, leaves),
        "forward_panel_1",
        [shaped(listed[1] * thin + 8, width)] * leaves,
        [room(spans[1], width), room(panel[1].shape[1], width)],
        6 * panel[1].size * width,
        2,
        meta,
        own_rows[1],
        *gather(solved[1]),
        panel[1],
    )
    pieces = to_leaves(pieces)
    piece = jnp.concatenate([sum(pieces[d : d + group]) for d in range(0, leaves, group)], axis=0)
    deferred = sum(deferred)
    own = scatter_chips(
        lambda k: jnp.concatenate([piece, lax.dynamic_index_in_dim(deferred, z ^ k, 0, False)], axis=0)
    )
    owed = call(
        functools.partial(owed_top_kernel, listed[1], thin),
        "owed_top",
        shaped(top_rows, width),
        [],
        0,
        1,
        meta,
        *own,
        *[to_core(item[: piece.shape[0]]) for item in own],
    )
    keep, send = call(
        functools.partial(forward_top_kernel, leaves),
        "forward_inv_0",
        halves(chunks[0]),
        [room(owned[0], width), room(spans[0], width)],
        6 * inv[0].size * width,
        1,
        meta,
        rhs[0],
        *to_leaves([owed] * leaves),
        inv[0],
    )
    solved[0] = scatter_sum(keep, send)

    parts = gather(solved[0])
    pieces = call(
        functools.partial(backward_top_kernel, len(parts), leaves),
        "backward_inv_0",
        [shaped(owned[0] // leaves, width)] * leaves,
        [room(spans[0], width), room(owned[0], width)],
        6 * inv[0].size * width,
        1,
        meta,
        *parts,
        inv[0],
    )
    piece = sum(to_leaves(pieces))
    quarters = gather(piece)
    top_parts = to_leaves([beside(piece, piece)] * leaves)

    def picked(levels, name, quarters, cost):
        picks = call(
            functools.partial(pick_kernel, len(quarters), leaves, [(helds[l], groups[l], listed[l]) for l in levels]),
            name,
            [shaped(sum(helds[l] * listed[l] for l in levels) * (BLOCK // leaves), width)] * leaves,
            [room(sizes[0] // leaves, width)],
            cost,
            1 + len(levels),
            meta,
            *[all_rows[l] for l in levels],
            *quarters,
        )
        return to_leaves(picks)

    blocks = owned[0] // BLOCK
    quarters, top_parts = lax.optimization_barrier((quarters, top_parts))
    top = jnp.zeros((blocks, leaves, thin, width), F32)
    for d, item in enumerate(top_parts):
        top = lax.dynamic_update_slice(top, item.reshape(blocks, 1, thin, width), (0, leaf ^ d, 0, 0))
    results = [top.reshape(rhs[0].shape)]
    picks = picked([1], "pick_1", quarters, 0)
    chain, parts = [], []
    for l in (1, 2, 3):
        above = sum(sizes[1:l])
        keep, send, *chain = call(
            functools.partial(
                backward_panel_kernel,
                len(parts),
                leaves,
                helds[l],
                sizes[0] // BLOCK,
                helds[2] * listed[2] * thin if l == 3 else 0,
                len(chain),
            ),
            f"backward_panel_{l}",
            halves(chunks[l]) + ([shaped(above, width)] if l > 1 else []),
            [
                room(panel[l].shape[1], width),
                pltpu.VMEM((panel[l].shape[1], 2 * width), BF16),
                room(spans[l], width),
            ],
            6 * panel[l].size * width,
            2,
            meta,
            own_rows[l],
            *picks,
            *parts,
            *chain,
            panel[l],
        )
        residue = solved[l] - scatter_sum(keep, send)
        if l == 1:
            picks = picked([2, 3], "pick_2_3", after(quarters, residue), BESIDE)
        x = call(
            backward_inv_kernel,
            f"backward_inv_{l}",
            shaped(helds[l], owned[l], width),
            [room(spans[l], width)],
            6 * inv[l].size * width,
            1,
            meta,
            *gather(residue),
            inv[l],
        )
        if l == 1:
            x, picks = lax.optimization_barrier((x, picks))
        x = leaf_sum(x, groups[l])
        if l < 3:
            parts = gather(x[0])
            placed = [x] + other_groups(beside(x, x), l)[1:]
            parts, placed = lax.optimization_barrier((parts, placed))
            results.append(place(placed, l))
    results.append(place(other_groups(x, 3), 3))
    return tuple(results)


def solution(mesh):
    across = P(None, "rows", None)
    return jax.shard_map(
        body,
        mesh=mesh,
        in_specs=(across,) * 4 + (P("rows", "leaf"),) * 4 + (P("leaf", "rows"),) * 3 + (P(None, "rows"),) * 3,
        out_specs=(across,) * 4,
        check_vma=False,
    )
```

```python
import functools

import jax
import jax.numpy as jnp
from jax import lax
from jax.experimental import pallas as pl
from jax.experimental.pallas import tpu as pltpu
from jax.sharding import PartitionSpec as P

BLOCK = 128
F32 = jnp.float32
BF16 = jnp.bfloat16
VMEM = pl.BlockSpec(memory_space=pltpu.VMEM)
SMEM = pl.BlockSpec(memory_space=pltpu.SMEM)
LIMIT = 14 * 1024 * 1024


def cut(x):
    high = x.astype(BF16)
    return high, (x - high.astype(F32)).astype(BF16)


def wide(x):
    return jnp.concatenate(cut(x), axis=1)


def product(dims, a, xw):
    n = xw.shape[1] // 2
    high, low = cut(a)
    first = lax.dot_general(high, xw, (dims, ((), ())), preferred_element_type=F32)
    second = lax.dot_general(low, xw[:, :n], (dims, ((), ())), preferred_element_type=F32)
    return first[:, :n] + (first[:, n:] + second)


times = functools.partial(product, ((1,), (0,)))
transposed_times = functools.partial(product, ((0,), (0,)))


def tile_of(rows, largest=512):
    return min(rows, largest)


def partners(count, rows):
    far_first = list(range(count - 1, 0, -1))
    return list(zip(far_first, far_first[-1:] + far_first[:-1] if rows >= 2 * BLOCK else far_first))


def spread_parts(meta, full, parts, offset=0):
    half = len(parts) // 2
    rows = parts[0].shape[0]
    steps = [(0, 0)] + partners(half, rows)
    for n, part in enumerate(parts):
        core = meta[1] if n < half else 1 - meta[1]
        first, second = steps[n % half]
        chip = jnp.bitwise_xor(meta[0], first + core * (second - first))
        full[pl.ds(pl.multiple_of(offset + (2 * chip + core) * rows, 8), rows), :] = part[...]


def split_cores(meta, full, offset, keep, send):
    count, rows = keep.shape[0], keep.shape[1]
    for k in range(count):
        keep[k] = full[pl.ds(pl.multiple_of(offset + (2 * k + meta[1]) * rows, 8), rows), :]
        send[k] = full[pl.ds(pl.multiple_of(offset + (2 * k + 1 - meta[1]) * rows, 8), rows), :]


def forward_inv_kernel(owed_count, meta, rhs, *refs):
    owed, inv, halves, full = refs[:owed_count], refs[owed_count], refs[owed_count + 1 : -1], refs[-1]
    held = rhs.shape[0]
    part = inv.shape[1] // held
    tile = tile_of(part)
    for h in range(held):
        source = rhs[h]
        for item in owed:
            source = source - item[...]
        source = wide(source)
        for start in range(h * part, (h + 1) * part, tile):
            full[start : start + tile, :] = transposed_times(inv[:, start : start + tile], source)
    split_cores(meta, full, 0, *halves)


def forward_top_kernel(leaves, meta, rhs, *refs):
    owed, (inv, keep, send, source, full) = refs[:leaves], refs[leaves:]
    height = BLOCK // leaves
    source[...] = rhs[0]
    for d in range(leaves):
        place = jnp.bitwise_xor(meta[2], d) * height
        for b in range(rhs.shape[1] // BLOCK):
            at = pl.ds(pl.multiple_of(b * BLOCK + place, 8), height)
            source[at, :] = source[at, :] - owed[d][b * height : (b + 1) * height, :]
    factor = wide(source[...])
    tile = tile_of(inv.shape[1])
    for start in range(0, inv.shape[1], tile):
        full[start : start + tile, :] = transposed_times(inv[:, start : start + tile], factor)
    split_cores(meta, full, 0, keep, send)


def panel_update(panel, full, h, held):
    part = panel.shape[0] // held
    tile = tile_of(part)
    update = None
    for start in range(h * part, (h + 1) * part, tile):
        term = transposed_times(panel[start : start + tile, :], wide(full[start : start + tile, :]))
        update = term if update is None else update + term
    return update


def add_blocks(chain, rows, updates, first):
    for k in range(rows.shape[0]):

        @pl.when(jnp.logical_and(rows[k] >= first, rows[k] < first + chain.shape[0] // BLOCK))
        def _(k=k):
            place = pl.ds(pl.multiple_of((rows[k] - first) * BLOCK, BLOCK), BLOCK)
            chain[place, :] = chain[place, :] + updates[k * BLOCK : (k + 1) * BLOCK, :]


def forward_panel_kernel(count, held, first, below_count, meta, rows, *refs):
    below_rows, refs = refs[:below_count], refs[below_count:]
    parts, refs = refs[:count], refs[count:]
    below, refs = refs[:below_count], refs[below_count:]
    panel, keep, send, updates, chain, full = refs
    size = updates.shape[0] // held
    spread_parts(meta, full, parts)
    for h in range(held):
        updates[h * size : (h + 1) * size, :] = panel_update(panel, full, h, held)
    chain[...] = jnp.zeros_like(chain)
    add_blocks(chain, rows, updates, first)
    for lower_rows, lower in zip(below_rows, below):
        add_blocks(chain, lower_rows, lower, first)
    split_cores(meta, chain, 0, keep, send)


def deferred_kernel(meta, upper_rows, lower_rows, upper, lower, keep, send, chain):
    leaves, count, rows = keep.shape[:3]
    height = BLOCK // leaves
    blocks = rows // height
    chain[...] = jnp.zeros_like(chain)
    add_blocks(chain, upper_rows, upper, 0)
    add_blocks(chain, lower_rows, lower, 0)
    for i in range(leaves):
        for k in range(count):
            for b in range(blocks):
                line = slice(b * height, (b + 1) * height)
                own = ((2 * k + meta[1]) * blocks + b) * BLOCK + i * height
                other = ((2 * k + 1 - meta[1]) * blocks + b) * BLOCK + i * height
                keep[i, k, line, :] = chain[pl.ds(pl.multiple_of(own, 8), height), :]
                send[i, k, line, :] = chain[pl.ds(pl.multiple_of(other, 8), height), :]


def leaf_cuts_kernel(meta, keep, received, dependency, *cuts):
    for d, cut in enumerate(cuts):
        other = jnp.bitwise_xor(meta[2], d)
        cut[...] = keep[other] + received[other]


def forward_last_kernel(nz, group, leaves, meta, rows, *refs):
    parts, refs = refs[: 2 * nz], refs[2 * nz :]
    panel, pieces, (full, update) = refs[0], refs[1:-2], refs[-2:]
    spread_parts(meta, full, parts)
    update[...] = panel_update(panel, full, 0, 1)
    listed = rows.shape[0]
    height = BLOCK // leaves
    for d in range(leaves):
        place = jnp.bitwise_xor(meta[2], d) * height
        for k in range(listed):
            at = pl.ds(pl.multiple_of(k * BLOCK + place, 8), height)
            pieces[d][k * height : (k + 1) * height, :] = update[at, :]
        tail = pieces[d].shape[0] - listed * height
        numbers = jnp.zeros((tail, update.shape[1]), F32)
        if d % group == 0:
            line = lax.broadcasted_iota(jnp.int32, numbers.shape, 0)
            for k in range(listed):
                numbers = jnp.where(line == k, rows[k].astype(F32), numbers)
        pieces[d][listed * height :, :] = numbers


def owed_top_kernel(listed, height, meta, *refs):
    parts, owed = refs[:-1], refs[-1]
    blocks = owed.shape[0] // height
    start = parts[-1].shape[0]
    size = listed * height + 8
    first = (2 * meta[0] + meta[1]) * blocks
    for b in range(blocks):
        wanted = (first + b).astype(F32)
        total = jnp.zeros((height, owed.shape[1]), F32)
        for item in parts:
            if item.shape[0] > start:
                total = total + item[start + b * height : start + (b + 1) * height, :]
            for at in range(0, start, size):
                for k in range(listed):
                    number = item[at + listed * height + k : at + listed * height + k + 1, :]
                    term = item[at + k * height : at + (k + 1) * height, :]
                    total = total + jnp.where(number == wanted, term, 0.0)
        owed[b * height : (b + 1) * height, :] = total


def pick_kernel(count, leaves, levels, meta, *refs):
    lists, refs = refs[: len(levels)], refs[len(levels) :]
    parts, picks, full = refs[:count], refs[count:-1], refs[-1]
    height = BLOCK // leaves
    last = full.shape[0] // height - 1
    spread_parts(meta, full, parts)
    for d in range(leaves):
        at = 0
        for (held, group, listed), rows in zip(levels, lists):
            first = jnp.bitwise_xor(meta[2], d) * held // group
            for h in range(held):
                for k in range(listed):
                    block = jnp.minimum(rows[(first + h) * listed + k], last)
                    picks[d][at : at + height, :] = full[pl.ds(pl.multiple_of(block * height, 8), height), :]
                    at += height


def backward_panel_kernel(count, leaves, held, top, skip, before_count, meta, rows, *refs):
    picks, refs = refs[:leaves], refs[leaves:]
    parts, refs = refs[:count], refs[count:]
    before, refs = refs[:before_count], refs[before_count:]
    panel, halves, chain, (chosen, factor, full) = refs[0], refs[1:3], refs[3:-3], refs[-3:]
    listed = rows.shape[0] // held
    height = BLOCK // leaves
    part = panel.shape[0] // held
    tile = tile_of(part)
    if chain:
        chain = chain[0]
        offset = 0
        if before:
            offset = before[0].shape[0]
            chain[:offset, :] = before[0][...]
        spread_parts(meta, chain, parts, offset)
    for h in range(held):
        for k in range(listed):
            for d in range(leaves):
                at = pl.ds(pl.multiple_of(k * BLOCK + jnp.bitwise_xor(meta[2], d) * height, 8), height)
                line = skip + (h * listed + k) * height
                chosen[at, :] = picks[d][line : line + height, :]
            if parts:

                @pl.when(rows[h * listed + k] >= top)
                def _(h=h, k=k):
                    place = pl.ds(pl.multiple_of((rows[h * listed + k] - top) * BLOCK, BLOCK), BLOCK)
                    chosen[k * BLOCK : (k + 1) * BLOCK, :] = chain[place, :]

        for k in range(listed):
            factor[k * BLOCK : (k + 1) * BLOCK, :] = wide(chosen[k * BLOCK : (k + 1) * BLOCK, :])
        for start in range(h * part, (h + 1) * part, tile):
            full[start : start + tile, :] = times(panel[start : start + tile, :], factor[...])
    split_cores(meta, full, 0, *halves)


def backward_sum(inv, full, h, held):
    part = inv.shape[1] // held
    tile = tile_of(part)
    total = None
    for start in range(h * part, (h + 1) * part, tile):
        term = times(inv[:, start : start + tile], wide(full[start : start + tile, :]))
        total = term if total is None else total + term
    return total


def backward_inv_kernel(meta, *refs):
    parts, (inv, solved, full) = refs[:-3], refs[-3:]
    spread_parts(meta, full, parts)
    for h in range(solved.shape[0]):
        solved[h] = backward_sum(inv, full, h, solved.shape[0])


def backward_top_kernel(count, leaves, meta, *refs):
    parts, refs = refs[:count], refs[count:]
    inv, pieces, (full, solved) = refs[0], refs[1:-2], refs[-2:]
    spread_parts(meta, full, parts)
    solved[...] = backward_sum(inv, full, 0, 1)
    height = BLOCK // leaves
    for d in range(leaves):
        place = jnp.bitwise_xor(meta[2], d) * height
        for b in range(solved.shape[0] // BLOCK):
            at = pl.ds(pl.multiple_of(b * BLOCK + place, 8), height)
            pieces[d][b * height : (b + 1) * height, :] = solved[at, :]


def call(kernel, name, out_shapes, scratch, flops, smem_count, *operands):
    single = not isinstance(out_shapes, (list, tuple))
    outs = [out_shapes] if single else list(out_shapes)
    moved = sum(item.size * 4 for item in operands) + sum(item.size * 4 for item in outs)
    result = pl.pallas_call(
        kernel,
        out_shape=outs,
        in_specs=[SMEM] * smem_count + [VMEM] * (len(operands) - smem_count),
        out_specs=[VMEM] * len(outs),
        scratch_shapes=scratch,
        compiler_params=pltpu.CompilerParams(vmem_limit_bytes=LIMIT),
        cost_estimate=pl.CostEstimate(flops=flops, bytes_accessed=moved, transcendentals=0),
        name=name,
    )(*operands)
    return result[0] if single else result


def spacer_kernel(x, dependency, out):
    out[...] = x[...]


BESIDE = 40_000_000_000


def beside(x, dependency):
    return pl.pallas_call(
        spacer_kernel,
        out_shape=jax.ShapeDtypeStruct(x.shape, x.dtype),
        in_specs=[VMEM, pl.BlockSpec(memory_space=pl.ANY)],
        out_specs=VMEM,
        compiler_params=pltpu.CompilerParams(vmem_limit_bytes=1024 * 1024),
        cost_estimate=pl.CostEstimate(flops=BESIDE, bytes_accessed=2 * x.size * 4, transcendentals=0),
        name="beside",
    )(x, dependency)


def shaped(*dims):
    return jax.ShapeDtypeStruct(dims, F32)


def after(x, *others):
    return lax.optimization_barrier((x, others))[0]


def body(*arguments):
    rhs, inv = arguments[0:4], arguments[4:8]
    panel, index_rows = (None,) + arguments[8:11], (None,) + arguments[11:14]
    leaves, devices = lax.axis_size("leaf"), lax.axis_size("rows")
    leaf, device = lax.axis_index("leaf"), lax.axis_index("rows")
    nz = devices // 2
    z, core = device // 2, device % 2
    meta = jnp.stack([z, core, leaf]).astype(jnp.int32)
    width = rhs[0].shape[2]
    owned = [item.shape[1] for item in rhs]
    sizes = [item * devices for item in owned]
    spans = [item.shape[1] for item in inv]
    helds = [max(1, spans[l] // sizes[l]) for l in range(4)]
    groups = [max(1, sizes[l] // spans[l]) for l in range(4)]
    chunks = [item // devices for item in spans]
    listed = [0] + [item.shape[1] // BLOCK for item in panel[1:]]

    def to_core(x):
        return lax.ppermute(x, "rows", [(r, r ^ 1) for r in range(devices)])

    def to_chip(x, step):
        return lax.ppermute(x, "rows", [(r, r ^ (2 * step[r % 2])) for r in range(devices)])

    def to_leaf(x, k):
        return x if k == 0 else lax.ppermute(x, "leaf", [(i, i ^ k) for i in range(leaves)])

    def to_leaves(pieces):
        far_first = {d: to_leaf(pieces[d], d) for d in reversed(range(len(pieces)))}
        return [far_first[d] for d in range(len(pieces))]

    def scatter_chips(chunk, steps):
        return [chunk(z)] + [to_chip(chunk(z ^ jnp.where(core == 0, step[0], step[1])), step) for step in steps]

    def scatter_parts(keep, send):
        received = to_core(send)
        return scatter_chips(
            lambda chip: lax.dynamic_index_in_dim(keep, chip, 0, False)
            + lax.dynamic_index_in_dim(received, chip, 0, False),
            partners(nz, keep.shape[1]),
        )

    def scatter_sum(keep, send):
        return sum(scatter_parts(keep, send))

    def gather(x):
        own = [x] + [to_chip(x, step) for step in partners(nz, x.shape[0])]
        return own + [to_core(item) for item in own]

    def leaf_sum(x, group):
        step = 1
        while step < group:
            x = x + to_leaf(x, step)
            step = step * 2
        return x

    def leaf_rows(x, l):
        return lax.dynamic_slice_in_dim(x, leaf * helds[l] // groups[l], helds[l], 0)

    def flat_rows(l, first, count):
        width_rows = index_rows[l].shape[1]
        at = lax.iota(jnp.int32, count * width_rows)[:, None, None]
        seps = lax.broadcasted_iota(jnp.int32, (1,) + index_rows[l].shape, 1)
        line = lax.broadcasted_iota(jnp.int32, (1,) + index_rows[l].shape, 2)
        wanted = (seps - first) * width_rows + line == at
        return jnp.sum(jnp.where(wanted, index_rows[l][None], 0), axis=(1, 2))

    def small_arrays():
        own = [flat_rows(l, leaf * helds[l] // groups[l], helds[l]) for l in (1, 2, 3)]
        every = [flat_rows(l, 0, index_rows[l].shape[0]) for l in (1, 2, 3)]
        return own, every, [leaf_rows(rhs[l], l) for l in (1, 2)]

    def other_groups(x, l):
        return [x] + [to_leaf(x, k * groups[l]) for k in range(1, leaves // groups[l])]

    def place(parts, l):
        out = jnp.zeros(rhs[l].shape, F32)
        for k, item in enumerate(parts):
            out = lax.dynamic_update_slice_in_dim(out, item, (leaf // groups[l] ^ k) * helds[l], 0)
        return out

    def halves(rows):
        return [shaped(nz, rows, width)] * 2

    def room(*dims):
        return pltpu.VMEM(dims, F32)

    def forward_inv(l, owed):
        return call(
            functools.partial(forward_inv_kernel, len(owed)),
            f"forward_inv_{l}",
            halves(chunks[l]),
            [room(spans[l], width)],
            6 * inv[l].size * width,
            1,
            meta,
            own_rhs[l],
            *owed,
            inv[l],
        )

    solved = [None] * 4

    own_rhs = [None, None, None, leaf_rows(rhs[3], 3)]
    parts = scatter_parts(*forward_inv(3, []))
    index_rows = (None,) + after(arguments[11:14], parts[0])
    parts, (own_rows, all_rows, early) = lax.optimization_barrier((parts, small_arrays()))
    own_rows, all_rows, own_rhs = [None] + own_rows, [None] + all_rows, [None] + early + own_rhs[3:]
    solved[3] = sum(parts)
    def forward_panel(l, below):
        parts = gather(solved[l])
        return call(
            functools.partial(forward_panel_kernel, len(parts), helds[l], sum(sizes[: l - 1]) // BLOCK, len(below)),
            f"forward_panel_{l}",
            halves(owned[l - 1]) + [shaped(helds[l] * listed[l] * BLOCK, width)],
            [room(sizes[l - 1], width), room(spans[l], width)],
            6 * panel[l].size * width,
            2 + len(below),
            meta,
            own_rows[l],
            *[own_rows[item] for item in below],
            *parts,
            *[updates[item] for item in below],
            panel[l],
        )

    updates = [None] * 4
    keep, send, updates[3] = forward_panel(3, [])

    def owed_parts(parts, l):
        if groups[l] == 1:
            return parts
        total = sum(parts)
        return [total, to_leaf(total, 1)] if groups[l] == 2 else [leaf_sum(total, groups[l])]

    solved[2] = scatter_sum(*forward_inv(2, owed_parts(scatter_parts(keep, send), 2)))
    keep, send, updates[2] = forward_panel(2, [3])
    parts = scatter_parts(keep, send)

    group, thin = groups[1], BLOCK // leaves
    top_rows = owned[0] // leaves
    top_keep, top_send = call(
        deferred_kernel,
        "deferred",
        [shaped(leaves, nz, top_rows, width)] * 2,
        [room(sizes[0], width)],
        0,
        3,
        meta,
        own_rows[2],
        own_rows[3],
        updates[2],
        updates[3],
    )
    leaf_cuts = call(
        leaf_cuts_kernel,
        "leaf_cuts",
        [shaped(nz, top_rows, width)] * leaves,
        [],
        BESIDE,
        1,
        meta,
        top_keep,
        to_core(top_send),
        parts[0],
    )
    deferred = to_leaves(leaf_cuts)
    solved[1] = scatter_sum(*forward_inv(1, owed_parts(parts, 1)))

    pieces = call(
        functools.partial(forward_last_kernel, nz, group, leaves),
        "forward_panel_1",
        [shaped(listed[1] * thin + 8, width)] * leaves,
        [room(spans[1], width), room(panel[1].shape[1], width)],
        6 * panel[1].size * width,
        2,
        meta,
        own_rows[1],
        *gather(solved[1]),
        panel[1],
    )
    pieces = to_leaves(pieces)
    piece = jnp.concatenate([sum(pieces[d : d + group]) for d in range(0, leaves, group)], axis=0)
    deferred = sum(deferred)
    own = scatter_chips(
        lambda chip: jnp.concatenate([piece, lax.dynamic_index_in_dim(deferred, chip, 0, False)], axis=0),
        partners(nz, piece.shape[0] + top_rows),
    )
    owed = call(
        functools.partial(owed_top_kernel, listed[1], thin),
        "owed_top",
        shaped(top_rows, width),
        [],
        0,
        1,
        meta,
        *own,
        *[to_core(item[: piece.shape[0]]) for item in own],
    )
    keep, send = call(
        functools.partial(forward_top_kernel, leaves),
        "forward_inv_0",
        halves(chunks[0]),
        [room(owned[0], width), room(spans[0], width)],
        6 * inv[0].size * width,
        1,
        meta,
        rhs[0],
        *to_leaves([owed] * leaves),
        inv[0],
    )
    solved[0] = scatter_sum(keep, send)

    parts = gather(solved[0])
    pieces = call(
        functools.partial(backward_top_kernel, len(parts), leaves),
        "backward_inv_0",
        [shaped(owned[0] // leaves, width)] * leaves,
        [room(spans[0], width), room(owned[0], width)],
        6 * inv[0].size * width,
        1,
        meta,
        *parts,
        inv[0],
    )
    piece = sum(to_leaves(pieces))
    quarters = gather(piece)
    top_parts = to_leaves([beside(piece, piece)] * leaves)

    def picked(levels, name, quarters, cost):
        picks = call(
            functools.partial(pick_kernel, len(quarters), leaves, [(helds[l], groups[l], listed[l]) for l in levels]),
            name,
            [shaped(sum(helds[l] * listed[l] for l in levels) * (BLOCK // leaves), width)] * leaves,
            [room(sizes[0] // leaves, width)],
            cost,
            1 + len(levels),
            meta,
            *[all_rows[l] for l in levels],
            *quarters,
        )
        return to_leaves(picks)

    blocks = owned[0] // BLOCK
    quarters, top_parts = lax.optimization_barrier((quarters, top_parts))
    top = jnp.zeros((blocks, leaves, thin, width), F32)
    for d, item in enumerate(top_parts):
        top = lax.dynamic_update_slice(top, item.reshape(blocks, 1, thin, width), (0, leaf ^ d, 0, 0))
    results = [top.reshape(rhs[0].shape)]
    picks = picked([1], "pick_1", quarters, 0)
    chain, parts = [], []
    for l in (1, 2, 3):
        above = sum(sizes[1:l])
        keep, send, *chain = call(
            functools.partial(
                backward_panel_kernel,
                len(parts),
                leaves,
                helds[l],
                sizes[0] // BLOCK,
                helds[2] * listed[2] * thin if l == 3 else 0,
                len(chain),
            ),
            f"backward_panel_{l}",
            halves(chunks[l]) + ([shaped(above, width)] if l > 1 else []),
            [
                room(panel[l].shape[1], width),
                pltpu.VMEM((panel[l].shape[1], 2 * width), BF16),
                room(spans[l], width),
            ],
            6 * panel[l].size * width,
            2,
            meta,
            own_rows[l],
            *picks,
            *parts,
            *chain,
            panel[l],
        )
        residue = solved[l] - scatter_sum(keep, send)
        if l == 1:
            picks = picked([2, 3], "pick_2_3", after(quarters, residue), BESIDE)
        x = call(
            backward_inv_kernel,
            f"backward_inv_{l}",
            shaped(helds[l], owned[l], width),
            [room(spans[l], width)],
            6 * inv[l].size * width,
            1,
            meta,
            *gather(residue),
            inv[l],
        )
        if l == 1:
            x, picks = lax.optimization_barrier((x, picks))
        x = leaf_sum(x, groups[l])
        if l < 3:
            parts = gather(x[0])
            placed = [x] + other_groups(beside(x, x), l)[1:]
            parts, placed = lax.optimization_barrier((parts, placed))
            results.append(place(placed, l))
    results.append(place(other_groups(x, 3), 3))
    return tuple(results)


def solution(mesh):
    across = P(None, "rows", None)
    return jax.shard_map(
        body,
        mesh=mesh,
        in_specs=(across,) * 4 + (P("rows", "leaf"),) * 4 + (P("leaf", "rows"),) * 3 + (P(None, "rows"),) * 3,
        out_specs=(across,) * 4,
        check_vma=False,
    )
```

```python
import functools

import jax
import jax.numpy as jnp
from jax import lax
from jax.experimental import pallas as pl
from jax.experimental.pallas import tpu as pltpu
from jax.sharding import PartitionSpec as P

BLOCK = 128
F32 = jnp.float32
BF16 = jnp.bfloat16
VMEM = pl.BlockSpec(memory_space=pltpu.VMEM)
SMEM = pl.BlockSpec(memory_space=pltpu.SMEM)
LIMIT = 14 * 1024 * 1024


def cut(x):
    high = x.astype(BF16)
    return high, (x - high.astype(F32)).astype(BF16)


def wide(x):
    return jnp.concatenate(cut(x), axis=1)


def product(dims, a, xw):
    n = xw.shape[1] // 2
    high, low = cut(a)
    first = lax.dot_general(high, xw, (dims, ((), ())), preferred_element_type=F32)
    second = lax.dot_general(low, xw[:, :n], (dims, ((), ())), preferred_element_type=F32)
    return first[:, :n] + (first[:, n:] + second)


times = functools.partial(product, ((1,), (0,)))
transposed_times = functools.partial(product, ((0,), (0,)))


def tile_of(rows, largest=512):
    return min(rows, largest)


def partners(count, rows):
    near_first = list(range(1, count))
    return list(zip(near_first, near_first[-1:] + near_first[:-1] if rows >= 2 * BLOCK else near_first))


def spread_parts(meta, full, parts, offset=0):
    half = len(parts) // 2
    rows = parts[0].shape[0]
    steps = [(0, 0)] + partners(half, rows)
    for n, part in enumerate(parts):
        core = meta[1] if n < half else 1 - meta[1]
        first, second = steps[n % half]
        chip = jnp.bitwise_xor(meta[0], first + core * (second - first))
        full[pl.ds(pl.multiple_of(offset + (2 * chip + core) * rows, 8), rows), :] = part[...]


def split_cores(meta, full, offset, keep, send):
    count, rows = keep.shape[0], keep.shape[1]
    for k in range(count):
        keep[k] = full[pl.ds(pl.multiple_of(offset + (2 * k + meta[1]) * rows, 8), rows), :]
        send[k] = full[pl.ds(pl.multiple_of(offset + (2 * k + 1 - meta[1]) * rows, 8), rows), :]


def forward_inv_kernel(owed_count, meta, rhs, *refs):
    owed, inv, halves, full = refs[:owed_count], refs[owed_count], refs[owed_count + 1 : -1], refs[-1]
    held = rhs.shape[0]
    part = inv.shape[1] // held
    tile = tile_of(part)
    for h in range(held):
        source = rhs[h]
        for item in owed:
            source = source - item[...]
        source = wide(source)
        for start in range(h * part, (h + 1) * part, tile):
            full[start : start + tile, :] = transposed_times(inv[:, start : start + tile], source)
    split_cores(meta, full, 0, *halves)


def forward_top_kernel(leaves, meta, rhs, *refs):
    owed, (inv, keep, send, source, full) = refs[:leaves], refs[leaves:]
    height = BLOCK // leaves
    source[...] = rhs[0]
    for d in range(leaves):
        place = jnp.bitwise_xor(meta[2], d) * height
        for b in range(rhs.shape[1] // BLOCK):
            at = pl.ds(pl.multiple_of(b * BLOCK + place, 8), height)
            source[at, :] = source[at, :] - owed[d][b * height : (b + 1) * height, :]
    factor = wide(source[...])
    tile = tile_of(inv.shape[1])
    for start in range(0, inv.shape[1], tile):
        full[start : start + tile, :] = transposed_times(inv[:, start : start + tile], factor)
    split_cores(meta, full, 0, keep, send)


def panel_update(panel, full, h, held):
    part = panel.shape[0] // held
    tile = tile_of(part)
    update = None
    for start in range(h * part, (h + 1) * part, tile):
        term = transposed_times(panel[start : start + tile, :], wide(full[start : start + tile, :]))
        update = term if update is None else update + term
    return update


def add_blocks(chain, rows, updates, first):
    for k in range(rows.shape[0]):

        @pl.when(jnp.logical_and(rows[k] >= first, rows[k] < first + chain.shape[0] // BLOCK))
        def _(k=k):
            place = pl.ds(pl.multiple_of((rows[k] - first) * BLOCK, BLOCK), BLOCK)
            chain[place, :] = chain[place, :] + updates[k * BLOCK : (k + 1) * BLOCK, :]


def forward_panel_kernel(count, held, first, below_count, meta, rows, *refs):
    below_rows, refs = refs[:below_count], refs[below_count:]
    parts, refs = refs[:count], refs[count:]
    below, refs = refs[:below_count], refs[below_count:]
    panel, keep, send, updates, chain, full = refs
    size = updates.shape[0] // held
    spread_parts(meta, full, parts)
    for h in range(held):
        updates[h * size : (h + 1) * size, :] = panel_update(panel, full, h, held)
    chain[...] = jnp.zeros_like(chain)
    add_blocks(chain, rows, updates, first)
    for lower_rows, lower in zip(below_rows, below):
        add_blocks(chain, lower_rows, lower, first)
    split_cores(meta, chain, 0, keep, send)


def deferred_kernel(meta, upper_rows, lower_rows, upper, lower, keep, send, chain):
    leaves, count, rows = keep.shape[:3]
    height = BLOCK // leaves
    blocks = rows // height
    chain[...] = jnp.zeros_like(chain)
    add_blocks(chain, upper_rows, upper, 0)
    add_blocks(chain, lower_rows, lower, 0)
    for i in range(leaves):
        for k in range(count):
            for b in range(blocks):
                line = slice(b * height, (b + 1) * height)
                own = ((2 * k + meta[1]) * blocks + b) * BLOCK + i * height
                other = ((2 * k + 1 - meta[1]) * blocks + b) * BLOCK + i * height
                keep[i, k, line, :] = chain[pl.ds(pl.multiple_of(own, 8), height), :]
                send[i, k, line, :] = chain[pl.ds(pl.multiple_of(other, 8), height), :]


def leaf_cuts_kernel(meta, keep, received, dependency, *cuts):
    for d, cut in enumerate(cuts):
        other = jnp.bitwise_xor(meta[2], d)
        cut[...] = keep[other] + received[other]


def forward_last_kernel(nz, group, leaves, meta, rows, *refs):
    parts, refs = refs[: 2 * nz], refs[2 * nz :]
    panel, pieces, (full, update) = refs[0], refs[1:-2], refs[-2:]
    spread_parts(meta, full, parts)
    update[...] = panel_update(panel, full, 0, 1)
    listed = rows.shape[0]
    height = BLOCK // leaves
    for d in range(leaves):
        place = jnp.bitwise_xor(meta[2], d) * height
        for k in range(listed):
            at = pl.ds(pl.multiple_of(k * BLOCK + place, 8), height)
            pieces[d][k * height : (k + 1) * height, :] = update[at, :]
        tail = pieces[d].shape[0] - listed * height
        numbers = jnp.zeros((tail, update.shape[1]), F32)
        if d % group == 0:
            line = lax.broadcasted_iota(jnp.int32, numbers.shape, 0)
            for k in range(listed):
                numbers = jnp.where(line == k, rows[k].astype(F32), numbers)
        pieces[d][listed * height :, :] = numbers


def owed_top_kernel(listed, height, meta, *refs):
    parts, (deferred, owed) = refs[:-2], refs[-2:]
    blocks = owed.shape[0] // height
    size = listed * height + 8
    first = (2 * meta[0] + meta[1]) * blocks
    for b in range(blocks):
        wanted = (first + b).astype(F32)
        total = deferred[b * height : (b + 1) * height, :]
        for item in parts:
            for at in range(0, item.shape[0], size):
                for k in range(listed):
                    number = item[at + listed * height + k : at + listed * height + k + 1, :]
                    term = item[at + k * height : at + (k + 1) * height, :]
                    total = total + jnp.where(number == wanted, term, 0.0)
        owed[b * height : (b + 1) * height, :] = total


def pick_kernel(count, leaves, levels, meta, *refs):
    lists, refs = refs[: len(levels)], refs[len(levels) :]
    parts, picks, full = refs[:count], refs[count:-1], refs[-1]
    height = BLOCK // leaves
    last = full.shape[0] // height - 1
    spread_parts(meta, full, parts)
    for d in range(leaves):
        at = 0
        for (held, group, listed), rows in zip(levels, lists):
            first = jnp.bitwise_xor(meta[2], d) * held // group
            for h in range(held):
                for k in range(listed):
                    block = jnp.minimum(rows[(first + h) * listed + k], last)
                    picks[d][at : at + height, :] = full[pl.ds(pl.multiple_of(block * height, 8), height), :]
                    at += height


def backward_panel_kernel(count, leaves, held, top, skip, before_count, meta, rows, *refs):
    picks, refs = refs[:leaves], refs[leaves:]
    parts, refs = refs[:count], refs[count:]
    before, refs = refs[:before_count], refs[before_count:]
    panel, halves, chain, (chosen, factor, full) = refs[0], refs[1:3], refs[3:-3], refs[-3:]
    listed = rows.shape[0] // held
    height = BLOCK // leaves
    part = panel.shape[0] // held
    tile = tile_of(part)
    if chain:
        chain = chain[0]
        offset = 0
        if before:
            offset = before[0].shape[0]
            chain[:offset, :] = before[0][...]
        spread_parts(meta, chain, parts, offset)
    for h in range(held):
        for k in range(listed):
            for d in range(leaves):
                at = pl.ds(pl.multiple_of(k * BLOCK + jnp.bitwise_xor(meta[2], d) * height, 8), height)
                line = skip + (h * listed + k) * height
                chosen[at, :] = picks[d][line : line + height, :]
            if parts:

                @pl.when(rows[h * listed + k] >= top)
                def _(h=h, k=k):
                    place = pl.ds(pl.multiple_of((rows[h * listed + k] - top) * BLOCK, BLOCK), BLOCK)
                    chosen[k * BLOCK : (k + 1) * BLOCK, :] = chain[place, :]

        for k in range(listed):
            factor[k * BLOCK : (k + 1) * BLOCK, :] = wide(chosen[k * BLOCK : (k + 1) * BLOCK, :])
        for start in range(h * part, (h + 1) * part, tile):
            full[start : start + tile, :] = times(panel[start : start + tile, :], factor[...])
    split_cores(meta, full, 0, *halves)


def backward_sum(inv, full, h, held):
    part = inv.shape[1] // held
    tile = tile_of(part)
    total = None
    for start in range(h * part, (h + 1) * part, tile):
        term = times(inv[:, start : start + tile], wide(full[start : start + tile, :]))
        total = term if total is None else total + term
    return total


def backward_inv_kernel(meta, *refs):
    parts, (inv, solved, full) = refs[:-3], refs[-3:]
    spread_parts(meta, full, parts)
    for h in range(solved.shape[0]):
        solved[h] = backward_sum(inv, full, h, solved.shape[0])


def backward_top_kernel(count, leaves, meta, *refs):
    parts, refs = refs[:count], refs[count:]
    inv, pieces, (full, solved) = refs[0], refs[1:-2], refs[-2:]
    spread_parts(meta, full, parts)
    solved[...] = backward_sum(inv, full, 0, 1)
    height = BLOCK // leaves
    for d in range(leaves):
        place = jnp.bitwise_xor(meta[2], d) * height
        for b in range(solved.shape[0] // BLOCK):
            at = pl.ds(pl.multiple_of(b * BLOCK + place, 8), height)
            pieces[d][b * height : (b + 1) * height, :] = solved[at, :]


def call(kernel, name, out_shapes, scratch, flops, smem_count, *operands):
    single = not isinstance(out_shapes, (list, tuple))
    outs = [out_shapes] if single else list(out_shapes)
    moved = sum(item.size * 4 for item in operands) + sum(item.size * 4 for item in outs)
    result = pl.pallas_call(
        kernel,
        out_shape=outs,
        in_specs=[SMEM] * smem_count + [VMEM] * (len(operands) - smem_count),
        out_specs=[VMEM] * len(outs),
        scratch_shapes=scratch,
        compiler_params=pltpu.CompilerParams(vmem_limit_bytes=LIMIT),
        cost_estimate=pl.CostEstimate(flops=flops, bytes_accessed=moved, transcendentals=0),
        name=name,
    )(*operands)
    return result[0] if single else result


def spacer_kernel(x, dependency, out):
    out[...] = x[...]


BESIDE = 40_000_000_000


def beside(x, dependency):
    return pl.pallas_call(
        spacer_kernel,
        out_shape=jax.ShapeDtypeStruct(x.shape, x.dtype),
        in_specs=[VMEM, pl.BlockSpec(memory_space=pl.ANY)],
        out_specs=VMEM,
        compiler_params=pltpu.CompilerParams(vmem_limit_bytes=1024 * 1024),
        cost_estimate=pl.CostEstimate(flops=BESIDE, bytes_accessed=2 * x.size * 4, transcendentals=0),
        name="beside",
    )(x, dependency)


def shaped(*dims):
    return jax.ShapeDtypeStruct(dims, F32)


def after(x, *others):
    return lax.optimization_barrier((x, others))[0]


def body(*arguments):
    rhs, inv = arguments[0:4], arguments[4:8]
    panel, index_rows = (None,) + arguments[8:11], (None,) + arguments[11:14]
    leaves, devices = lax.axis_size("leaf"), lax.axis_size("rows")
    leaf, device = lax.axis_index("leaf"), lax.axis_index("rows")
    nz = devices // 2
    z, core = device // 2, device % 2
    meta = jnp.stack([z, core, leaf]).astype(jnp.int32)
    width = rhs[0].shape[2]
    owned = [item.shape[1] for item in rhs]
    sizes = [item * devices for item in owned]
    spans = [item.shape[1] for item in inv]
    helds = [max(1, spans[l] // sizes[l]) for l in range(4)]
    groups = [max(1, sizes[l] // spans[l]) for l in range(4)]
    chunks = [item // devices for item in spans]
    listed = [0] + [item.shape[1] // BLOCK for item in panel[1:]]

    def to_core(x):
        return lax.ppermute(x, "rows", [(r, r ^ 1) for r in range(devices)])

    def to_chip(x, step):
        return lax.ppermute(x, "rows", [(r, r ^ (2 * step[r % 2])) for r in range(devices)])

    def to_leaf(x, k):
        return x if k == 0 else lax.ppermute(x, "leaf", [(i, i ^ k) for i in range(leaves)])

    def to_leaves(pieces):
        far_first = {d: to_leaf(pieces[d], d) for d in reversed(range(len(pieces)))}
        return [far_first[d] for d in range(len(pieces))]

    def scatter_chips(chunk, steps):
        return [chunk(z)] + [to_chip(chunk(z ^ jnp.where(core == 0, step[0], step[1])), step) for step in steps]

    def scatter_parts(keep, send):
        received = to_core(send)
        return scatter_chips(
            lambda chip: lax.dynamic_index_in_dim(keep, chip, 0, False)
            + lax.dynamic_index_in_dim(received, chip, 0, False),
            partners(nz, keep.shape[1]),
        )

    def scatter_sum(keep, send):
        return sum(scatter_parts(keep, send))

    def gather(x):
        own = [x] + [to_chip(x, step) for step in partners(nz, x.shape[0])]
        return own + [to_core(item) for item in own]

    def leaf_sum(x, group):
        step = 1
        while step < group:
            x = x + to_leaf(x, step)
            step = step * 2
        return x

    def leaf_rows(x, l):
        return lax.dynamic_slice_in_dim(x, leaf * helds[l] // groups[l], helds[l], 0)

    def flat_rows(l, first, count):
        width_rows = index_rows[l].shape[1]
        at = lax.iota(jnp.int32, count * width_rows)[:, None, None]
        seps = lax.broadcasted_iota(jnp.int32, (1,) + index_rows[l].shape, 1)
        line = lax.broadcasted_iota(jnp.int32, (1,) + index_rows[l].shape, 2)
        wanted = (seps - first) * width_rows + line == at
        return jnp.sum(jnp.where(wanted, index_rows[l][None], 0), axis=(1, 2))

    def small_arrays():
        own = [flat_rows(l, leaf * helds[l] // groups[l], helds[l]) for l in (1, 2, 3)]
        every = [flat_rows(l, 0, index_rows[l].shape[0]) for l in (1, 2, 3)]
        return own, every, [leaf_rows(rhs[l], l) for l in (1, 2)]

    def other_groups(x, l):
        return [x] + [to_leaf(x, k * groups[l]) for k in range(1, leaves // groups[l])]

    def place(parts, l):
        out = jnp.zeros(rhs[l].shape, F32)
        for k, item in enumerate(parts):
            out = lax.dynamic_update_slice_in_dim(out, item, (leaf // groups[l] ^ k) * helds[l], 0)
        return out

    def halves(rows):
        return [shaped(nz, rows, width)] * 2

    def room(*dims):
        return pltpu.VMEM(dims, F32)

    def forward_inv(l, owed):
        return call(
            functools.partial(forward_inv_kernel, len(owed)),
            f"forward_inv_{l}",
            halves(chunks[l]),
            [room(spans[l], width)],
            6 * inv[l].size * width,
            1,
            meta,
            own_rhs[l],
            *owed,
            inv[l],
        )

    solved = [None] * 4

    own_rhs = [None, None, None, leaf_rows(rhs[3], 3)]
    parts = scatter_parts(*forward_inv(3, []))
    index_rows = (None,) + after(arguments[11:14], parts[0])
    parts, (own_rows, all_rows, early) = lax.optimization_barrier((parts, small_arrays()))
    own_rows, all_rows, own_rhs = [None] + own_rows, [None] + all_rows, [None] + early + own_rhs[3:]
    solved[3] = sum(parts)
    def forward_panel(l, below):
        parts = gather(solved[l])
        return call(
            functools.partial(forward_panel_kernel, len(parts), helds[l], sum(sizes[: l - 1]) // BLOCK, len(below)),
            f"forward_panel_{l}",
            halves(owned[l - 1]) + [shaped(helds[l] * listed[l] * BLOCK, width)],
            [room(sizes[l - 1], width), room(spans[l], width)],
            6 * panel[l].size * width,
            2 + len(below),
            meta,
            own_rows[l],
            *[own_rows[item] for item in below],
            *parts,
            *[updates[item] for item in below],
            panel[l],
        )

    updates = [None] * 4
    keep, send, updates[3] = forward_panel(3, [])

    def owed_parts(parts, l):
        if groups[l] == 1:
            return parts
        total = sum(parts)
        return [total, to_leaf(total, 1)] if groups[l] == 2 else [leaf_sum(total, groups[l])]

    solved[2] = scatter_sum(*forward_inv(2, owed_parts(scatter_parts(keep, send), 2)))
    keep, send, updates[2] = forward_panel(2, [3])
    parts = scatter_parts(keep, send)

    group, thin = groups[1], BLOCK // leaves
    top_rows = owned[0] // leaves
    top_keep, top_send = call(
        deferred_kernel,
        "deferred",
        [shaped(leaves, nz, top_rows, width)] * 2,
        [room(sizes[0], width)],
        0,
        3,
        meta,
        own_rows[2],
        own_rows[3],
        updates[2],
        updates[3],
    )
    leaf_cuts = call(
        leaf_cuts_kernel,
        "leaf_cuts",
        [shaped(nz, top_rows, width)] * leaves,
        [],
        BESIDE,
        1,
        meta,
        top_keep,
        to_core(top_send),
        parts[0],
    )
    deferred = to_leaves(leaf_cuts)
    solved[1] = scatter_sum(*forward_inv(1, owed_parts(parts, 1)))
    parts, deferred = lax.optimization_barrier((gather(solved[1]), deferred))

    pieces = call(
        functools.partial(forward_last_kernel, nz, group, leaves),
        "forward_panel_1",
        [shaped(listed[1] * thin + 8, width)] * leaves,
        [room(spans[1], width), room(panel[1].shape[1], width)],
        6 * panel[1].size * width,
        2,
        meta,
        own_rows[1],
        *parts,
        panel[1],
    )
    own_piece = pieces[0]
    pieces = to_leaves(pieces)
    piece = jnp.concatenate([sum(pieces[d : d + group]) for d in range(0, leaves, group)], axis=0)
    deferred = beside(sum(deferred), own_piece)
    deferred = scatter_chips(
        lambda chip: lax.dynamic_index_in_dim(deferred, chip, 0, False), partners(nz, top_rows)
    )
    owed = call(
        functools.partial(owed_top_kernel, listed[1], thin),
        "owed_top",
        shaped(top_rows, width),
        [],
        0,
        1,
        meta,
        *gather(piece),
        sum(deferred),
    )
    keep, send = call(
        functools.partial(forward_top_kernel, leaves),
        "forward_inv_0",
        halves(chunks[0]),
        [room(owned[0], width), room(spans[0], width)],
        6 * inv[0].size * width,
        1,
        meta,
        rhs[0],
        *to_leaves([owed] * leaves),
        inv[0],
    )
    solved[0] = scatter_sum(keep, send)

    parts = gather(solved[0])
    pieces = call(
        functools.partial(backward_top_kernel, len(parts), leaves),
        "backward_inv_0",
        [shaped(owned[0] // leaves, width)] * leaves,
        [room(spans[0], width), room(owned[0], width)],
        6 * inv[0].size * width,
        1,
        meta,
        *parts,
        inv[0],
    )
    piece = sum(to_leaves(pieces))
    quarters = gather(piece)
    top_parts = to_leaves([beside(piece, piece)] * leaves)

    def picked(levels, name, quarters, cost):
        picks = call(
            functools.partial(pick_kernel, len(quarters), leaves, [(helds[l], groups[l], listed[l]) for l in levels]),
            name,
            [shaped(sum(helds[l] * listed[l] for l in levels) * (BLOCK // leaves), width)] * leaves,
            [room(sizes[0] // leaves, width)],
            cost,
            1 + len(levels),
            meta,
            *[all_rows[l] for l in levels],
            *quarters,
        )
        return to_leaves(picks)

    blocks = owned[0] // BLOCK
    quarters, top_parts = lax.optimization_barrier((quarters, top_parts))
    top = jnp.zeros((blocks, leaves, thin, width), F32)
    for d, item in enumerate(top_parts):
        top = lax.dynamic_update_slice(top, item.reshape(blocks, 1, thin, width), (0, leaf ^ d, 0, 0))
    results = [top.reshape(rhs[0].shape)]
    picks = picked([1], "pick_1", quarters, 0)
    chain, parts = [], []
    for l in (1, 2, 3):
        above = sum(sizes[1:l])
        keep, send, *chain = call(
            functools.partial(
                backward_panel_kernel,
                len(parts),
                leaves,
                helds[l],
                sizes[0] // BLOCK,
                helds[2] * listed[2] * thin if l == 3 else 0,
                len(chain),
            ),
            f"backward_panel_{l}",
            halves(chunks[l]) + ([shaped(above, width)] if l > 1 else []),
            [
                room(panel[l].shape[1], width),
                pltpu.VMEM((panel[l].shape[1], 2 * width), BF16),
                room(spans[l], width),
            ],
            6 * panel[l].size * width,
            2,
            meta,
            own_rows[l],
            *picks,
            *parts,
            *chain,
            panel[l],
        )
        residue = solved[l] - scatter_sum(keep, send)
        if l == 1:
            picks = picked([2, 3], "pick_2_3", after(quarters, residue), BESIDE)
        x = call(
            backward_inv_kernel,
            f"backward_inv_{l}",
            shaped(helds[l], owned[l], width),
            [room(spans[l], width)],
            6 * inv[l].size * width,
            1,
            meta,
            *gather(residue),
            inv[l],
        )
        if l == 1:
            x, picks = lax.optimization_barrier((x, picks))
        x = leaf_sum(x, groups[l])
        if l < 3:
            parts = gather(x[0])
            placed = [x] + other_groups(beside(x, x), l)[1:]
            parts, placed = lax.optimization_barrier((parts, placed))
            results.append(place(placed, l))
    results.append(place(other_groups(x, 3), 3))
    return tuple(results)


def solution(mesh):
    across = P(None, "rows", None)
    return jax.shard_map(
        body,
        mesh=mesh,
        in_specs=(across,) * 4 + (P("rows", "leaf"),) * 4 + (P("leaf", "rows"),) * 3 + (P(None, "rows"),) * 3,
        out_specs=(across,) * 4,
        check_vma=False,
    )
```

```python
import functools

import jax
import jax.numpy as jnp
from jax import lax
from jax.experimental import pallas as pl
from jax.experimental.pallas import tpu as pltpu
from jax.sharding import PartitionSpec as P

BLOCK = 128
F32 = jnp.float32
BF16 = jnp.bfloat16
VMEM = pl.BlockSpec(memory_space=pltpu.VMEM)
SMEM = pl.BlockSpec(memory_space=pltpu.SMEM)
LIMIT = 14 * 1024 * 1024


def cut(x):
    high = x.astype(BF16)
    return high, (x - high.astype(F32)).astype(BF16)


def wide(x):
    return jnp.concatenate(cut(x), axis=1)


def product(dims, a, xw):
    n = xw.shape[1] // 2
    high, low = cut(a)
    first = lax.dot_general(high, xw, (dims, ((), ())), preferred_element_type=F32)
    second = lax.dot_general(low, xw[:, :n], (dims, ((), ())), preferred_element_type=F32)
    return first[:, :n] + (first[:, n:] + second)


times = functools.partial(product, ((1,), (0,)))
transposed_times = functools.partial(product, ((0,), (0,)))


def tile_of(rows, largest=512):
    return min(rows, largest)


def partners(count, rows):
    near_first = list(range(1, count))
    return list(zip(near_first, near_first[-1:] + near_first[:-1] if rows >= 2 * BLOCK else near_first))


def spread_parts(meta, full, parts, offset=0):
    half = len(parts) // 2
    rows = parts[0].shape[0]
    steps = [(0, 0)] + partners(half, rows)
    for n, part in enumerate(parts):
        core = meta[1] if n < half else 1 - meta[1]
        first, second = steps[n % half]
        chip = jnp.bitwise_xor(meta[0], first + core * (second - first))
        full[pl.ds(pl.multiple_of(offset + (2 * chip + core) * rows, 8), rows), :] = part[...]


def split_cores(meta, full, offset, keep, send):
    count, rows = keep.shape[0], keep.shape[1]
    for k in range(count):
        keep[k] = full[pl.ds(pl.multiple_of(offset + (2 * k + meta[1]) * rows, 8), rows), :]
        send[k] = full[pl.ds(pl.multiple_of(offset + (2 * k + 1 - meta[1]) * rows, 8), rows), :]


def forward_inv_kernel(owed_count, meta, rhs, *refs):
    owed, inv, halves, full = refs[:owed_count], refs[owed_count], refs[owed_count + 1 : -1], refs[-1]
    held = rhs.shape[0]
    part = inv.shape[1] // held
    tile = tile_of(part)
    for h in range(held):
        source = rhs[h]
        for item in owed:
            source = source - item[...]
        source = wide(source)
        for start in range(h * part, (h + 1) * part, tile):
            full[start : start + tile, :] = transposed_times(inv[:, start : start + tile], source)
    split_cores(meta, full, 0, *halves)


def forward_top_kernel(leaves, meta, rhs, *refs):
    owed, (inv, keep, send, source, full) = refs[:leaves], refs[leaves:]
    height = BLOCK // leaves
    source[...] = rhs[0]
    for d in range(leaves):
        place = jnp.bitwise_xor(meta[2], d) * height
        for b in range(rhs.shape[1] // BLOCK):
            at = pl.ds(pl.multiple_of(b * BLOCK + place, 8), height)
            source[at, :] = source[at, :] - owed[d][b * height : (b + 1) * height, :]
    factor = wide(source[...])
    tile = tile_of(inv.shape[1])
    for start in range(0, inv.shape[1], tile):
        full[start : start + tile, :] = transposed_times(inv[:, start : start + tile], factor)
    split_cores(meta, full, 0, keep, send)


def panel_update(panel, full, h, held):
    part = panel.shape[0] // held
    tile = tile_of(part)
    update = None
    for start in range(h * part, (h + 1) * part, tile):
        term = transposed_times(panel[start : start + tile, :], wide(full[start : start + tile, :]))
        update = term if update is None else update + term
    return update


def add_blocks(chain, rows, updates, first):
    for k in range(rows.shape[0]):

        @pl.when(jnp.logical_and(rows[k] >= first, rows[k] < first + chain.shape[0] // BLOCK))
        def _(k=k):
            place = pl.ds(pl.multiple_of((rows[k] - first) * BLOCK, BLOCK), BLOCK)
            chain[place, :] = chain[place, :] + updates[k * BLOCK : (k + 1) * BLOCK, :]


def forward_panel_kernel(count, held, first, below_count, meta, rows, *refs):
    below_rows, refs = refs[:below_count], refs[below_count:]
    parts, refs = refs[:count], refs[count:]
    below, refs = refs[:below_count], refs[below_count:]
    panel, keep, send, updates, chain, full = refs
    size = updates.shape[0] // held
    spread_parts(meta, full, parts)
    for h in range(held):
        updates[h * size : (h + 1) * size, :] = panel_update(panel, full, h, held)
    chain[...] = jnp.zeros_like(chain)
    add_blocks(chain, rows, updates, first)
    for lower_rows, lower in zip(below_rows, below):
        add_blocks(chain, lower_rows, lower, first)
    split_cores(meta, chain, 0, keep, send)


def deferred_kernel(meta, upper_rows, lower_rows, upper, lower, keep, send, chain):
    leaves, count, rows = keep.shape[:3]
    height = BLOCK // leaves
    blocks = rows // height
    chain[...] = jnp.zeros_like(chain)
    add_blocks(chain, upper_rows, upper, 0)
    add_blocks(chain, lower_rows, lower, 0)
    for i in range(leaves):
        for k in range(count):
            for b in range(blocks):
                line = slice(b * height, (b + 1) * height)
                own = ((2 * k + meta[1]) * blocks + b) * BLOCK + i * height
                other = ((2 * k + 1 - meta[1]) * blocks + b) * BLOCK + i * height
                keep[i, k, line, :] = chain[pl.ds(pl.multiple_of(own, 8), height), :]
                send[i, k, line, :] = chain[pl.ds(pl.multiple_of(other, 8), height), :]


def leaf_cuts_kernel(meta, keep, received, dependency, *cuts):
    for d, cut in enumerate(cuts):
        other = jnp.bitwise_xor(meta[2], d)
        cut[...] = keep[other] + received[other]


def forward_last_kernel(nz, group, leaves, meta, rows, *refs):
    parts, refs = refs[: 2 * nz], refs[2 * nz :]
    panel, pieces, (full, update) = refs[0], refs[1:-2], refs[-2:]
    spread_parts(meta, full, parts)
    update[...] = panel_update(panel, full, 0, 1)
    listed = rows.shape[0]
    height = BLOCK // leaves
    for d in range(leaves):
        place = jnp.bitwise_xor(meta[2], d) * height
        for k in range(listed):
            at = pl.ds(pl.multiple_of(k * BLOCK + place, 8), height)
            pieces[d][k * height : (k + 1) * height, :] = update[at, :]
        tail = pieces[d].shape[0] - listed * height
        numbers = jnp.zeros((tail, update.shape[1]), F32)
        if d % group == 0:
            line = lax.broadcasted_iota(jnp.int32, numbers.shape, 0)
            for k in range(listed):
                numbers = jnp.where(line == k, rows[k].astype(F32), numbers)
        pieces[d][listed * height :, :] = numbers


def owed_top_kernel(listed, height, meta, *refs):
    parts, (deferred, owed) = refs[:-2], refs[-2:]
    blocks = owed.shape[0] // height
    size = listed * height + 8
    first = (2 * meta[0] + meta[1]) * blocks
    for b in range(blocks):
        wanted = (first + b).astype(F32)
        total = deferred[b * height : (b + 1) * height, :]
        for item in parts:
            for at in range(0, item.shape[0], size):
                for k in range(listed):
                    number = item[at + listed * height + k : at + listed * height + k + 1, :]
                    term = item[at + k * height : at + (k + 1) * height, :]
                    total = total + jnp.where(number == wanted, term, 0.0)
        owed[b * height : (b + 1) * height, :] = total


def pick_kernel(count, leaves, levels, meta, *refs):
    lists, refs = refs[: len(levels)], refs[len(levels) :]
    parts, picks, full = refs[:count], refs[count:-1], refs[-1]
    height = BLOCK // leaves
    last = full.shape[0] // height - 1
    spread_parts(meta, full, parts)
    for d in range(leaves):
        at = 0
        for (held, group, listed), rows in zip(levels, lists):
            first = jnp.bitwise_xor(meta[2], d) * held // group
            for h in range(held):
                for k in range(listed):
                    block = jnp.minimum(rows[(first + h) * listed + k], last)
                    picks[d][at : at + height, :] = full[pl.ds(pl.multiple_of(block * height, 8), height), :]
                    at += height


def backward_panel_kernel(count, leaves, held, top, skip, before_count, meta, rows, *refs):
    picks, refs = refs[:leaves], refs[leaves:]
    parts, refs = refs[:count], refs[count:]
    before, refs = refs[:before_count], refs[before_count:]
    panel, halves, chain, (chosen, factor, full) = refs[0], refs[1:3], refs[3:-3], refs[-3:]
    listed = rows.shape[0] // held
    height = BLOCK // leaves
    part = panel.shape[0] // held
    tile = tile_of(part)
    if chain:
        chain = chain[0]
        offset = 0
        if before:
            offset = before[0].shape[0]
            chain[:offset, :] = before[0][...]
        spread_parts(meta, chain, parts, offset)
    for h in range(held):
        for k in range(listed):
            for d in range(leaves):
                at = pl.ds(pl.multiple_of(k * BLOCK + jnp.bitwise_xor(meta[2], d) * height, 8), height)
                line = skip + (h * listed + k) * height
                chosen[at, :] = picks[d][line : line + height, :]
            if parts:

                @pl.when(rows[h * listed + k] >= top)
                def _(h=h, k=k):
                    place = pl.ds(pl.multiple_of((rows[h * listed + k] - top) * BLOCK, BLOCK), BLOCK)
                    chosen[k * BLOCK : (k + 1) * BLOCK, :] = chain[place, :]

        for k in range(listed):
            factor[k * BLOCK : (k + 1) * BLOCK, :] = wide(chosen[k * BLOCK : (k + 1) * BLOCK, :])
        for start in range(h * part, (h + 1) * part, tile):
            full[start : start + tile, :] = times(panel[start : start + tile, :], factor[...])
    split_cores(meta, full, 0, *halves)


def backward_sum(inv, full, h, held):
    part = inv.shape[1] // held
    tile = tile_of(part)
    total = None
    for start in range(h * part, (h + 1) * part, tile):
        term = times(inv[:, start : start + tile], wide(full[start : start + tile, :]))
        total = term if total is None else total + term
    return total


def backward_inv_kernel(meta, *refs):
    parts, (inv, solved, full) = refs[:-3], refs[-3:]
    spread_parts(meta, full, parts)
    for h in range(solved.shape[0]):
        solved[h] = backward_sum(inv, full, h, solved.shape[0])


def backward_top_kernel(count, leaves, meta, *refs):
    parts, refs = refs[:count], refs[count:]
    inv, pieces, (full, solved) = refs[0], refs[1:-2], refs[-2:]
    spread_parts(meta, full, parts)
    solved[...] = backward_sum(inv, full, 0, 1)
    height = BLOCK // leaves
    for d in range(leaves):
        place = jnp.bitwise_xor(meta[2], d) * height
        for b in range(solved.shape[0] // BLOCK):
            at = pl.ds(pl.multiple_of(b * BLOCK + place, 8), height)
            pieces[d][b * height : (b + 1) * height, :] = solved[at, :]


def call(kernel, name, out_shapes, scratch, flops, smem_count, *operands):
    single = not isinstance(out_shapes, (list, tuple))
    outs = [out_shapes] if single else list(out_shapes)
    moved = sum(item.size * 4 for item in operands) + sum(item.size * 4 for item in outs)
    result = pl.pallas_call(
        kernel,
        out_shape=outs,
        in_specs=[SMEM] * smem_count + [VMEM] * (len(operands) - smem_count),
        out_specs=[VMEM] * len(outs),
        scratch_shapes=scratch,
        compiler_params=pltpu.CompilerParams(vmem_limit_bytes=LIMIT),
        cost_estimate=pl.CostEstimate(flops=flops, bytes_accessed=moved, transcendentals=0),
        name=name,
    )(*operands)
    return result[0] if single else result


def spacer_kernel(x, dependency, out):
    out[...] = x[...]


BESIDE = 40_000_000_000


def beside(x, dependency):
    return pl.pallas_call(
        spacer_kernel,
        out_shape=jax.ShapeDtypeStruct(x.shape, x.dtype),
        in_specs=[VMEM, pl.BlockSpec(memory_space=pl.ANY)],
        out_specs=VMEM,
        compiler_params=pltpu.CompilerParams(vmem_limit_bytes=1024 * 1024),
        cost_estimate=pl.CostEstimate(flops=BESIDE, bytes_accessed=2 * x.size * 4, transcendentals=0),
        name="beside",
    )(x, dependency)


def shaped(*dims):
    return jax.ShapeDtypeStruct(dims, F32)


def after(x, *others):
    return lax.optimization_barrier((x, others))[0]


def body(*arguments):
    rhs, inv = arguments[0:4], arguments[4:8]
    panel, index_rows = (None,) + arguments[8:11], (None,) + arguments[11:14]
    leaves, devices = lax.axis_size("leaf"), lax.axis_size("rows")
    leaf, device = lax.axis_index("leaf"), lax.axis_index("rows")
    nz = devices // 2
    z, core = device // 2, device % 2
    meta = jnp.stack([z, core, leaf]).astype(jnp.int32)
    width = rhs[0].shape[2]
    owned = [item.shape[1] for item in rhs]
    sizes = [item * devices for item in owned]
    spans = [item.shape[1] for item in inv]
    helds = [max(1, spans[l] // sizes[l]) for l in range(4)]
    groups = [max(1, sizes[l] // spans[l]) for l in range(4)]
    chunks = [item // devices for item in spans]
    listed = [0] + [item.shape[1] // BLOCK for item in panel[1:]]

    def to_core(x):
        return lax.ppermute(x, "rows", [(r, r ^ 1) for r in range(devices)])

    def to_chip(x, step):
        return lax.ppermute(x, "rows", [(r, r ^ (2 * step[r % 2])) for r in range(devices)])

    def to_leaf(x, k):
        return x if k == 0 else lax.ppermute(x, "leaf", [(i, i ^ k) for i in range(leaves)])

    def to_leaves(pieces):
        far_first = {d: to_leaf(pieces[d], d) for d in reversed(range(len(pieces)))}
        return [far_first[d] for d in range(len(pieces))]

    known = {}

    def chip_index(step):
        return known[step] if step in known else (z ^ jnp.where(core == 0, step[0], step[1])).astype(jnp.uint32)

    def leaf_index(group, k):
        return known[group, k, "leaf"] if known else (leaf // group ^ k).astype(jnp.uint32)

    def small_indices():
        steps = [(0, 0)] + partners(nz, BLOCK) + partners(nz, 2 * BLOCK)
        found = {step: chip_index(step) for step in steps}
        for group in {1, *groups}:
            found.update({(group, k, "leaf"): leaf_index(group, k) for k in range(leaves // group)})
        return list(found), list(found.values())

    def scatter_chips(chunk, steps):
        return [chunk(chip_index((0, 0)))] + [to_chip(chunk(chip_index(step)), step) for step in steps]

    def scatter_parts(keep, send):
        received = to_core(send)
        return scatter_chips(
            lambda chip: lax.dynamic_index_in_dim(keep, chip, 0, False)
            + lax.dynamic_index_in_dim(received, chip, 0, False),
            partners(nz, keep.shape[1]),
        )

    def scatter_sum(keep, send):
        return sum(scatter_parts(keep, send))

    def gather(x):
        own = [x] + [to_chip(x, step) for step in partners(nz, x.shape[0])]
        return own + [to_core(item) for item in own]

    def leaf_sum(x, group):
        step = 1
        while step < group:
            x = x + to_leaf(x, step)
            step = step * 2
        return x

    def leaf_rows(x, l):
        return lax.dynamic_slice_in_dim(x, leaf * helds[l] // groups[l], helds[l], 0)

    def flat_rows(l, first, count):
        width_rows = index_rows[l].shape[1]
        at = lax.iota(jnp.int32, count * width_rows)[:, None, None]
        seps = lax.broadcasted_iota(jnp.int32, (1,) + index_rows[l].shape, 1)
        line = lax.broadcasted_iota(jnp.int32, (1,) + index_rows[l].shape, 2)
        wanted = (seps - first) * width_rows + line == at
        return jnp.sum(jnp.where(wanted, index_rows[l][None], 0), axis=(1, 2))

    def small_arrays():
        own = [flat_rows(l, leaf * helds[l] // groups[l], helds[l]) for l in (1, 2, 3)]
        every = [flat_rows(l, 0, index_rows[l].shape[0]) for l in (1, 2, 3)]
        return own, every, [leaf_rows(rhs[l], l) for l in (1, 2)]

    def other_groups(x, l):
        return [x] + [to_leaf(x, k * groups[l]) for k in range(1, leaves // groups[l])]

    def place(parts, l):
        out = jnp.zeros(rhs[l].shape, F32)
        for k, item in enumerate(parts):
            out = lax.dynamic_update_slice_in_dim(out, item, leaf_index(groups[l], k) * helds[l], 0)
        return out

    def halves(rows):
        return [shaped(nz, rows, width)] * 2

    def room(*dims):
        return pltpu.VMEM(dims, F32)

    def forward_inv(l, owed):
        return call(
            functools.partial(forward_inv_kernel, len(owed)),
            f"forward_inv_{l}",
            halves(chunks[l]),
            [room(spans[l], width)],
            6 * inv[l].size * width,
            1,
            meta,
            own_rhs[l],
            *owed,
            inv[l],
        )

    solved = [None] * 4

    own_rhs = [None, None, None, leaf_rows(rhs[3], 3)]
    parts = scatter_parts(*forward_inv(3, []))
    index_rows = (None,) + after(arguments[11:14], parts[0])
    names, places = small_indices()
    parts, (own_rows, all_rows, early), places = lax.optimization_barrier((parts, small_arrays(), places))
    known.update(zip(names, places))
    own_rows, all_rows, own_rhs = [None] + own_rows, [None] + all_rows, [None] + early + own_rhs[3:]
    solved[3] = sum(parts)
    def forward_panel(l, below):
        parts = gather(solved[l])
        return call(
            functools.partial(forward_panel_kernel, len(parts), helds[l], sum(sizes[: l - 1]) // BLOCK, len(below)),
            f"forward_panel_{l}",
            halves(owned[l - 1]) + [shaped(helds[l] * listed[l] * BLOCK, width)],
            [room(sizes[l - 1], width), room(spans[l], width)],
            6 * panel[l].size * width,
            2 + len(below),
            meta,
            own_rows[l],
            *[own_rows[item] for item in below],
            *parts,
            *[updates[item] for item in below],
            panel[l],
        )

    updates = [None] * 4
    keep, send, updates[3] = forward_panel(3, [])

    def owed_parts(parts, l):
        if groups[l] == 1:
            return parts
        total = sum(parts)
        return [total, to_leaf(total, 1)] if groups[l] == 2 else [leaf_sum(total, groups[l])]

    solved[2] = scatter_sum(*forward_inv(2, owed_parts(scatter_parts(keep, send), 2)))
    keep, send, updates[2] = forward_panel(2, [3])
    parts = scatter_parts(keep, send)

    group, thin = groups[1], BLOCK // leaves
    top_rows = owned[0] // leaves
    top_keep, top_send = call(
        deferred_kernel,
        "deferred",
        [shaped(leaves, nz, top_rows, width)] * 2,
        [room(sizes[0], width)],
        0,
        3,
        meta,
        own_rows[2],
        own_rows[3],
        updates[2],
        updates[3],
    )
    leaf_cuts = call(
        leaf_cuts_kernel,
        "leaf_cuts",
        [shaped(nz, top_rows, width)] * leaves,
        [],
        BESIDE,
        1,
        meta,
        top_keep,
        to_core(top_send),
        parts[0],
    )
    deferred = to_leaves(leaf_cuts)
    solved[1] = scatter_sum(*forward_inv(1, owed_parts(parts, 1)))
    parts, deferred = lax.optimization_barrier((gather(solved[1]), deferred))

    pieces = call(
        functools.partial(forward_last_kernel, nz, group, leaves),
        "forward_panel_1",
        [shaped(listed[1] * thin + 8, width)] * leaves,
        [room(spans[1], width), room(panel[1].shape[1], width)],
        6 * panel[1].size * width,
        2,
        meta,
        own_rows[1],
        *parts,
        panel[1],
    )
    own_piece = pieces[0]
    pieces = to_leaves(pieces)
    piece = jnp.concatenate([sum(pieces[d : d + group]) for d in range(0, leaves, group)], axis=0)
    deferred = beside(sum(deferred), own_piece)
    deferred = scatter_chips(
        lambda chip: lax.dynamic_index_in_dim(deferred, chip, 0, False), partners(nz, top_rows)
    )
    owed = call(
        functools.partial(owed_top_kernel, listed[1], thin),
        "owed_top",
        shaped(top_rows, width),
        [],
        0,
        1,
        meta,
        *gather(piece),
        sum(deferred),
    )
    keep, send = call(
        functools.partial(forward_top_kernel, leaves),
        "forward_inv_0",
        halves(chunks[0]),
        [room(owned[0], width), room(spans[0], width)],
        6 * inv[0].size * width,
        1,
        meta,
        rhs[0],
        *to_leaves([owed] * leaves),
        inv[0],
    )
    solved[0] = scatter_sum(keep, send)

    parts = gather(solved[0])
    pieces = call(
        functools.partial(backward_top_kernel, len(parts), leaves),
        "backward_inv_0",
        [shaped(owned[0] // leaves, width)] * leaves,
        [room(spans[0], width), room(owned[0], width)],
        6 * inv[0].size * width,
        1,
        meta,
        *parts,
        inv[0],
    )
    piece = sum(to_leaves(pieces))
    quarters = gather(piece)
    top_parts = to_leaves([beside(piece, piece)] * leaves)

    def picked(levels, name, quarters, cost):
        picks = call(
            functools.partial(pick_kernel, len(quarters), leaves, [(helds[l], groups[l], listed[l]) for l in levels]),
            name,
            [shaped(sum(helds[l] * listed[l] for l in levels) * (BLOCK // leaves), width)] * leaves,
            [room(sizes[0] // leaves, width)],
            cost,
            1 + len(levels),
            meta,
            *[all_rows[l] for l in levels],
            *quarters,
        )
        return to_leaves(picks)

    blocks = owned[0] // BLOCK
    quarters, top_parts = lax.optimization_barrier((quarters, top_parts))
    top, zero = jnp.zeros((blocks, leaves, thin, width), F32), jnp.uint32(0)
    for d, item in enumerate(top_parts):
        top = lax.dynamic_update_slice(top, item.reshape(blocks, 1, thin, width), (zero, leaf_index(1, d), zero, zero))
    results = [top.reshape(rhs[0].shape)]
    picks = picked([1], "pick_1", quarters, 0)
    chain, parts = [], []
    for l in (1, 2, 3):
        above = sum(sizes[1:l])
        keep, send, *chain = call(
            functools.partial(
                backward_panel_kernel,
                len(parts),
                leaves,
                helds[l],
                sizes[0] // BLOCK,
                helds[2] * listed[2] * thin if l == 3 else 0,
                len(chain),
            ),
            f"backward_panel_{l}",
            halves(chunks[l]) + ([shaped(above, width)] if l > 1 else []),
            [
                room(panel[l].shape[1], width),
                pltpu.VMEM((panel[l].shape[1], 2 * width), BF16),
                room(spans[l], width),
            ],
            6 * panel[l].size * width,
            2,
            meta,
            own_rows[l],
            *picks,
            *parts,
            *chain,
            panel[l],
        )
        residue = solved[l] - scatter_sum(keep, send)
        if l == 1:
            picks = picked([2, 3], "pick_2_3", after(quarters, residue), BESIDE)
        x = call(
            backward_inv_kernel,
            f"backward_inv_{l}",
            shaped(helds[l], owned[l], width),
            [room(spans[l], width)],
            6 * inv[l].size * width,
            1,
            meta,
            *gather(residue),
            inv[l],
        )
        if l == 1:
            x, picks = lax.optimization_barrier((x, picks))
        x = leaf_sum(x, groups[l])
        if l < 3:
            parts = gather(x[0])
            placed = [x] + other_groups(beside(x, x), l)[1:]
            parts, placed = lax.optimization_barrier((parts, placed))
            results.append(place(placed, l))
    results.append(place(other_groups(x, 3), 3))
    return tuple(results)


def solution(mesh):
    across = P(None, "rows", None)
    return jax.shard_map(
        body,
        mesh=mesh,
        in_specs=(across,) * 4 + (P("rows", "leaf"),) * 4 + (P("leaf", "rows"),) * 3 + (P(None, "rows"),) * 3,
        out_specs=(across,) * 4,
        check_vma=False,
    )
```

```python
import functools

import jax
import jax.numpy as jnp
from jax import lax
from jax.experimental import pallas as pl
from jax.experimental.pallas import tpu as pltpu
from jax.sharding import PartitionSpec as P

BLOCK = 128
F32 = jnp.float32
BF16 = jnp.bfloat16
VMEM = pl.BlockSpec(memory_space=pltpu.VMEM)
SMEM = pl.BlockSpec(memory_space=pltpu.SMEM)
LIMIT = 14 * 1024 * 1024


def cut(x):
    high = x.astype(BF16)
    return high, (x - high.astype(F32)).astype(BF16)


def wide(x):
    return jnp.concatenate(cut(x), axis=1)


def product(dims, a, xw):
    n = xw.shape[1] // 2
    high, low = cut(a)
    first = lax.dot_general(high, xw, (dims, ((), ())), preferred_element_type=F32)
    second = lax.dot_general(low, xw[:, :n], (dims, ((), ())), preferred_element_type=F32)
    return first[:, :n] + (first[:, n:] + second)


times = functools.partial(product, ((1,), (0,)))
transposed_times = functools.partial(product, ((0,), (0,)))


def tile_of(rows, largest=512):
    return min(rows, largest)


def partners(count, rows):
    near_first = list(range(1, count))
    return list(zip(near_first, near_first[-1:] + near_first[:-1] if rows >= 2 * BLOCK else near_first))


def spread_parts(meta, full, parts, offset=0):
    half = len(parts) // 2
    rows = parts[0].shape[0]
    steps = [(0, 0)] + partners(half, rows)
    for n, part in enumerate(parts):
        core = meta[1] if n < half else 1 - meta[1]
        first, second = steps[n % half]
        chip = jnp.bitwise_xor(meta[0], first + core * (second - first))
        full[pl.ds(pl.multiple_of(offset + (2 * chip + core) * rows, 8), rows), :] = part[...]


def split_cores(meta, full, offset, keep, send):
    count, rows = keep.shape[0], keep.shape[1]
    for k in range(count):
        keep[k] = full[pl.ds(pl.multiple_of(offset + (2 * k + meta[1]) * rows, 8), rows), :]
        send[k] = full[pl.ds(pl.multiple_of(offset + (2 * k + 1 - meta[1]) * rows, 8), rows), :]


def forward_inv_kernel(owed_count, meta, rhs, *refs):
    owed, inv, halves, full = refs[:owed_count], refs[owed_count], refs[owed_count + 1 : -1], refs[-1]
    held = rhs.shape[0]
    part = inv.shape[1] // held
    tile = tile_of(part)
    for h in range(held):
        source = rhs[h]
        for item in owed:
            source = source - item[...]
        source = wide(source)
        for start in range(h * part, (h + 1) * part, tile):
            full[start : start + tile, :] = transposed_times(inv[:, start : start + tile], source)
    split_cores(meta, full, 0, *halves)


def forward_top_kernel(leaves, meta, rhs, *refs):
    owed, (inv, keep, send, source, full) = refs[:leaves], refs[leaves:]
    height = BLOCK // leaves
    source[...] = rhs[0]
    for d in range(leaves):
        place = jnp.bitwise_xor(meta[2], d) * height
        for b in range(rhs.shape[1] // BLOCK):
            at = pl.ds(pl.multiple_of(b * BLOCK + place, 8), height)
            source[at, :] = source[at, :] - owed[d][b * height : (b + 1) * height, :]
    factor = wide(source[...])
    tile = tile_of(inv.shape[1])
    for start in range(0, inv.shape[1], tile):
        full[start : start + tile, :] = transposed_times(inv[:, start : start + tile], factor)
    split_cores(meta, full, 0, keep, send)


def panel_update(panel, full, h, held):
    part = panel.shape[0] // held
    tile = tile_of(part)
    update = None
    for start in range(h * part, (h + 1) * part, tile):
        term = transposed_times(panel[start : start + tile, :], wide(full[start : start + tile, :]))
        update = term if update is None else update + term
    return update


def add_blocks(chain, rows, updates, first):
    for k in range(rows.shape[0]):

        @pl.when(jnp.logical_and(rows[k] >= first, rows[k] < first + chain.shape[0] // BLOCK))
        def _(k=k):
            place = pl.ds(pl.multiple_of((rows[k] - first) * BLOCK, BLOCK), BLOCK)
            chain[place, :] = chain[place, :] + updates[k * BLOCK : (k + 1) * BLOCK, :]


def forward_panel_kernel(count, held, first, below_count, meta, rows, *refs):
    below_rows, refs = refs[:below_count], refs[below_count:]
    parts, refs = refs[:count], refs[count:]
    below, refs = refs[:below_count], refs[below_count:]
    panel, keep, send, updates, chain, full = refs
    size = updates.shape[0] // held
    spread_parts(meta, full, parts)
    for h in range(held):
        updates[h * size : (h + 1) * size, :] = panel_update(panel, full, h, held)
    chain[...] = jnp.zeros_like(chain)
    add_blocks(chain, rows, updates, first)
    for lower_rows, lower in zip(below_rows, below):
        add_blocks(chain, lower_rows, lower, first)
    split_cores(meta, chain, 0, keep, send)


def deferred_kernel(meta, upper_rows, lower_rows, upper, lower, keep, send, chain):
    leaves, count, rows = keep.shape[:3]
    height = BLOCK // leaves
    blocks = rows // height
    chain[...] = jnp.zeros_like(chain)
    add_blocks(chain, upper_rows, upper, 0)
    add_blocks(chain, lower_rows, lower, 0)
    for i in range(leaves):
        for k in range(count):
            for b in range(blocks):
                line = slice(b * height, (b + 1) * height)
                own = ((2 * k + meta[1]) * blocks + b) * BLOCK + i * height
                other = ((2 * k + 1 - meta[1]) * blocks + b) * BLOCK + i * height
                keep[i, k, line, :] = chain[pl.ds(pl.multiple_of(own, 8), height), :]
                send[i, k, line, :] = chain[pl.ds(pl.multiple_of(other, 8), height), :]


def leaf_cuts_kernel(meta, keep, received, dependency, *cuts):
    for d, cut in enumerate(cuts):
        other = jnp.bitwise_xor(meta[2], d)
        cut[...] = keep[other] + received[other]


def forward_last_kernel(nz, group, leaves, meta, rows, *refs):
    parts, refs = refs[: 2 * nz], refs[2 * nz :]
    panel, pieces, (full, update) = refs[0], refs[1:-2], refs[-2:]
    spread_parts(meta, full, parts)
    update[...] = panel_update(panel, full, 0, 1)
    listed = rows.shape[0]
    height = BLOCK // leaves
    for d in range(leaves):
        place = jnp.bitwise_xor(meta[2], d) * height
        for k in range(listed):
            at = pl.ds(pl.multiple_of(k * BLOCK + place, 8), height)
            pieces[d][k * height : (k + 1) * height, :] = update[at, :]
        tail = pieces[d].shape[0] - listed * height
        numbers = jnp.zeros((tail, update.shape[1]), F32)
        if d % group == 0:
            line = lax.broadcasted_iota(jnp.int32, numbers.shape, 0)
            for k in range(listed):
                numbers = jnp.where(line == k, rows[k].astype(F32), numbers)
        pieces[d][listed * height :, :] = numbers


def owed_top_kernel(listed, height, meta, *refs):
    parts, (deferred, owed) = refs[:-2], refs[-2:]
    blocks = owed.shape[0] // height
    size = listed * height + 8
    first = (2 * meta[0] + meta[1]) * blocks
    for b in range(blocks):
        wanted = (first + b).astype(F32)
        total = deferred[b * height : (b + 1) * height, :]
        for item in parts:
            for at in range(0, item.shape[0], size):
                for k in range(listed):
                    number = item[at + listed * height + k : at + listed * height + k + 1, :]
                    term = item[at + k * height : at + (k + 1) * height, :]
                    total = total + jnp.where(number == wanted, term, 0.0)
        owed[b * height : (b + 1) * height, :] = total


def pick_kernel(count, leaves, levels, meta, *refs):
    lists, refs = refs[: len(levels)], refs[len(levels) :]
    parts, picks, full = refs[:count], refs[count:-1], refs[-1]
    height = BLOCK // leaves
    last = full.shape[0] // height - 1
    spread_parts(meta, full, parts)
    for d in range(leaves):
        at = 0
        for (held, group, listed), rows in zip(levels, lists):
            first = jnp.bitwise_xor(meta[2], d) * held // group
            for h in range(held):
                for k in range(listed):
                    block = jnp.minimum(rows[(first + h) * listed + k], last)
                    picks[d][at : at + height, :] = full[pl.ds(pl.multiple_of(block * height, 8), height), :]
                    at += height


def backward_panel_kernel(count, leaves, held, top, skip, before_count, meta, rows, *refs):
    picks, refs = refs[:leaves], refs[leaves:]
    parts, refs = refs[:count], refs[count:]
    before, refs = refs[:before_count], refs[before_count:]
    panel, halves, chain, (chosen, factor, full) = refs[0], refs[1:3], refs[3:-3], refs[-3:]
    listed = rows.shape[0] // held
    height = BLOCK // leaves
    part = panel.shape[0] // held
    tile = tile_of(part)
    if chain:
        chain = chain[0]
        offset = 0
        if before:
            offset = before[0].shape[0]
            chain[:offset, :] = before[0][...]
        spread_parts(meta, chain, parts, offset)
    for h in range(held):
        for k in range(listed):
            for d in range(leaves):
                at = pl.ds(pl.multiple_of(k * BLOCK + jnp.bitwise_xor(meta[2], d) * height, 8), height)
                line = skip + (h * listed + k) * height
                chosen[at, :] = picks[d][line : line + height, :]
            if parts:

                @pl.when(rows[h * listed + k] >= top)
                def _(h=h, k=k):
                    place = pl.ds(pl.multiple_of((rows[h * listed + k] - top) * BLOCK, BLOCK), BLOCK)
                    chosen[k * BLOCK : (k + 1) * BLOCK, :] = chain[place, :]

        for k in range(listed):
            factor[k * BLOCK : (k + 1) * BLOCK, :] = wide(chosen[k * BLOCK : (k + 1) * BLOCK, :])
        for start in range(h * part, (h + 1) * part, tile):
            full[start : start + tile, :] = times(panel[start : start + tile, :], factor[...])
    split_cores(meta, full, 0, *halves)


def backward_sum(inv, full, h, held):
    part = inv.shape[1] // held
    tile = tile_of(part)
    total = None
    for start in range(h * part, (h + 1) * part, tile):
        term = times(inv[:, start : start + tile], wide(full[start : start + tile, :]))
        total = term if total is None else total + term
    return total


def backward_inv_kernel(meta, *refs):
    parts, (inv, solved, full) = refs[:-3], refs[-3:]
    spread_parts(meta, full, parts)
    for h in range(solved.shape[0]):
        solved[h] = backward_sum(inv, full, h, solved.shape[0])


def backward_top_kernel(count, leaves, meta, *refs):
    parts, refs = refs[:count], refs[count:]
    inv, pieces, (full, solved) = refs[0], refs[1:-2], refs[-2:]
    spread_parts(meta, full, parts)
    solved[...] = backward_sum(inv, full, 0, 1)
    height = BLOCK // leaves
    for d in range(leaves):
        place = jnp.bitwise_xor(meta[2], d) * height
        for b in range(solved.shape[0] // BLOCK):
            at = pl.ds(pl.multiple_of(b * BLOCK + place, 8), height)
            pieces[d][b * height : (b + 1) * height, :] = solved[at, :]


def call(kernel, name, out_shapes, scratch, flops, smem_count, *operands):
    single = not isinstance(out_shapes, (list, tuple))
    outs = [out_shapes] if single else list(out_shapes)
    moved = sum(item.size * 4 for item in operands) + sum(item.size * 4 for item in outs)
    result = pl.pallas_call(
        kernel,
        out_shape=outs,
        in_specs=[SMEM] * smem_count + [VMEM] * (len(operands) - smem_count),
        out_specs=[VMEM] * len(outs),
        scratch_shapes=scratch,
        compiler_params=pltpu.CompilerParams(vmem_limit_bytes=LIMIT),
        cost_estimate=pl.CostEstimate(flops=flops, bytes_accessed=moved, transcendentals=0),
        name=name,
    )(*operands)
    return result[0] if single else result


def spacer_kernel(x, dependency, out):
    out[...] = x[...]


BESIDE = 40_000_000_000


def beside(x, dependency):
    return pl.pallas_call(
        spacer_kernel,
        out_shape=jax.ShapeDtypeStruct(x.shape, x.dtype),
        in_specs=[VMEM, pl.BlockSpec(memory_space=pl.ANY)],
        out_specs=VMEM,
        compiler_params=pltpu.CompilerParams(vmem_limit_bytes=1024 * 1024),
        cost_estimate=pl.CostEstimate(flops=BESIDE, bytes_accessed=2 * x.size * 4, transcendentals=0),
        name="beside",
    )(x, dependency)


def shaped(*dims):
    return jax.ShapeDtypeStruct(dims, F32)


def after(x, *others):
    return lax.optimization_barrier((x, others))[0]


def body(*arguments):
    rhs, inv = arguments[0:4], arguments[4:8]
    panel, index_rows = (None,) + arguments[8:11], (None,) + arguments[11:14]
    leaves, devices = lax.axis_size("leaf"), lax.axis_size("rows")
    leaf, device = lax.axis_index("leaf"), lax.axis_index("rows")
    nz = devices // 2
    z, core = device // 2, device % 2
    meta = jnp.stack([z, core, leaf]).astype(jnp.int32)
    width = rhs[0].shape[2]
    owned = [item.shape[1] for item in rhs]
    sizes = [item * devices for item in owned]
    spans = [item.shape[1] for item in inv]
    helds = [max(1, spans[l] // sizes[l]) for l in range(4)]
    groups = [max(1, sizes[l] // spans[l]) for l in range(4)]
    chunks = [item // devices for item in spans]
    listed = [0] + [item.shape[1] // BLOCK for item in panel[1:]]

    def to_core(x):
        return lax.ppermute(x, "rows", [(r, r ^ 1) for r in range(devices)])

    def to_chip(x, step):
        return lax.ppermute(x, "rows", [(r, r ^ (2 * step[r % 2])) for r in range(devices)])

    def to_leaf(x, k):
        return x if k == 0 else lax.ppermute(x, "leaf", [(i, i ^ k) for i in range(leaves)])

    def to_leaves(pieces):
        far_first = {d: to_leaf(pieces[d], d) for d in reversed(range(len(pieces)))}
        return [far_first[d] for d in range(len(pieces))]

    known = {}

    def chip_index(step):
        return known[step] if step in known else (z ^ jnp.where(core == 0, step[0], step[1])).astype(jnp.uint32)

    def leaf_index(group, k):
        return known[group, k, "leaf"] if known else (leaf // group ^ k).astype(jnp.uint32)

    def small_indices():
        steps = [(0, 0)] + partners(nz, BLOCK) + partners(nz, 2 * BLOCK)
        found = {step: chip_index(step) for step in steps}
        for group in {1, *groups}:
            found.update({(group, k, "leaf"): leaf_index(group, k) for k in range(leaves // group)})
        return list(found), list(found.values())

    def scatter_chips(chunk, steps):
        return [chunk(chip_index((0, 0)))] + [to_chip(chunk(chip_index(step)), step) for step in steps]

    def scatter_parts(keep, send):
        received = to_core(send)
        return scatter_chips(
            lambda chip: lax.dynamic_index_in_dim(keep, chip, 0, False)
            + lax.dynamic_index_in_dim(received, chip, 0, False),
            partners(nz, keep.shape[1]),
        )

    def scatter_sum(keep, send):
        return sum(scatter_parts(keep, send))

    def gather(x):
        own = [x] + [to_chip(x, step) for step in partners(nz, x.shape[0])]
        return own + [to_core(item) for item in own]

    def leaf_sum(x, group):
        step = 1
        while step < group:
            x = x + to_leaf(x, step)
            step = step * 2
        return x

    def leaf_rows(x, l):
        return lax.dynamic_slice_in_dim(x, leaf * helds[l] // groups[l], helds[l], 0)

    def flat_rows(l, first, count):
        width_rows = index_rows[l].shape[1]
        at = lax.iota(jnp.int32, count * width_rows)[:, None, None]
        seps = lax.broadcasted_iota(jnp.int32, (1,) + index_rows[l].shape, 1)
        line = lax.broadcasted_iota(jnp.int32, (1,) + index_rows[l].shape, 2)
        wanted = (seps - first) * width_rows + line == at
        return jnp.sum(jnp.where(wanted, index_rows[l][None], 0), axis=(1, 2))

    def small_arrays():
        own = [flat_rows(l, leaf * helds[l] // groups[l], helds[l]) for l in (1, 2, 3)]
        every = [flat_rows(l, 0, index_rows[l].shape[0]) for l in (1, 2, 3)]
        return own, every, [leaf_rows(rhs[l], l) for l in (1, 2)]

    def other_groups(x, l):
        return [x] + [to_leaf(x, k * groups[l]) for k in range(1, leaves // groups[l])]

    def place(parts, l):
        out = jnp.zeros(rhs[l].shape, F32)
        for k, item in enumerate(parts):
            out = lax.dynamic_update_slice_in_dim(out, item, leaf_index(groups[l], k) * helds[l], 0)
        return out

    def halves(rows):
        return [shaped(nz, rows, width)] * 2

    def room(*dims):
        return pltpu.VMEM(dims, F32)

    def forward_inv(l, owed):
        return call(
            functools.partial(forward_inv_kernel, len(owed)),
            f"forward_inv_{l}",
            halves(chunks[l]),
            [room(spans[l], width)],
            6 * inv[l].size * width,
            1,
            meta,
            own_rhs[l],
            *owed,
            inv[l],
        )

    solved = [None] * 4

    own_rhs = [None, None, None, leaf_rows(rhs[3], 3)]
    parts = scatter_parts(*forward_inv(3, []))
    index_rows = (None,) + after(arguments[11:14], parts[0])
    names, places = small_indices()
    parts, (own_rows, all_rows, early), places = lax.optimization_barrier((parts, small_arrays(), places))
    known.update(zip(names, places))
    own_rows, all_rows, own_rhs = [None] + own_rows, [None] + all_rows, [None] + early + own_rhs[3:]
    solved[3] = sum(parts)
    def forward_panel(l, below):
        parts = gather(solved[l])
        return call(
            functools.partial(forward_panel_kernel, len(parts), helds[l], sum(sizes[: l - 1]) // BLOCK, len(below)),
            f"forward_panel_{l}",
            halves(owned[l - 1]) + [shaped(helds[l] * listed[l] * BLOCK, width)],
            [room(sizes[l - 1], width), room(spans[l], width)],
            6 * panel[l].size * width,
            2 + len(below),
            meta,
            own_rows[l],
            *[own_rows[item] for item in below],
            *parts,
            *[updates[item] for item in below],
            panel[l],
        )

    updates = [None] * 4
    keep, send, updates[3] = forward_panel(3, [])

    def owed_parts(parts, l):
        if groups[l] == 1:
            return parts
        total = sum(parts)
        return [total, to_leaf(total, 1)] if groups[l] == 2 else [leaf_sum(total, groups[l])]

    solved[2] = scatter_sum(*forward_inv(2, owed_parts(scatter_parts(keep, send), 2)))
    keep, send, updates[2] = forward_panel(2, [3])
    parts = scatter_parts(keep, send)

    group, thin = groups[1], BLOCK // leaves
    top_rows = owned[0] // leaves
    top_keep, top_send = call(
        deferred_kernel,
        "deferred",
        [shaped(leaves, nz, top_rows, width)] * 2,
        [room(sizes[0], width)],
        0,
        3,
        meta,
        own_rows[2],
        own_rows[3],
        updates[2],
        updates[3],
    )
    leaf_cuts = call(
        leaf_cuts_kernel,
        "leaf_cuts",
        [shaped(nz, top_rows, width)] * leaves,
        [],
        BESIDE,
        1,
        meta,
        top_keep,
        to_core(top_send),
        parts[0],
    )
    deferred = to_leaves(leaf_cuts)
    solved[1] = scatter_sum(*forward_inv(1, owed_parts(parts, 1)))
    parts, deferred = lax.optimization_barrier((gather(solved[1]), deferred))

    pieces = call(
        functools.partial(forward_last_kernel, nz, group, leaves),
        "forward_panel_1",
        [shaped(listed[1] * thin + 8, width)] * leaves,
        [room(spans[1], width), room(panel[1].shape[1], width)],
        6 * panel[1].size * width,
        2,
        meta,
        own_rows[1],
        *parts,
        panel[1],
    )
    own_piece = pieces[0]
    pieces = to_leaves(pieces)
    piece = jnp.concatenate([sum(pieces[d : d + group]) for d in range(0, leaves, group)], axis=0)
    deferred = beside(sum(deferred), own_piece)
    deferred = scatter_chips(
        lambda chip: lax.dynamic_index_in_dim(deferred, chip, 0, False), partners(nz, top_rows)
    )
    owed = call(
        functools.partial(owed_top_kernel, listed[1], thin),
        "owed_top",
        shaped(top_rows, width),
        [],
        0,
        1,
        meta,
        *gather(piece),
        sum(deferred),
    )
    keep, send = call(
        functools.partial(forward_top_kernel, leaves),
        "forward_inv_0",
        halves(chunks[0]),
        [room(owned[0], width), room(spans[0], width)],
        6 * inv[0].size * width,
        1,
        meta,
        rhs[0],
        *to_leaves([owed] * leaves),
        inv[0],
    )
    solved[0] = scatter_sum(keep, send)

    parts = gather(solved[0])
    pieces = call(
        functools.partial(backward_top_kernel, len(parts), leaves),
        "backward_inv_0",
        [shaped(owned[0] // leaves, width)] * leaves,
        [room(spans[0], width), room(owned[0], width)],
        6 * inv[0].size * width,
        1,
        meta,
        *parts,
        inv[0],
    )
    piece = sum(to_leaves(pieces))
    quarters = gather(piece)
    top_parts = to_leaves([beside(piece, piece)] * leaves)

    def picked(levels, name, quarters, cost):
        picks = call(
            functools.partial(pick_kernel, len(quarters), leaves, [(helds[l], groups[l], listed[l]) for l in levels]),
            name,
            [shaped(sum(helds[l] * listed[l] for l in levels) * (BLOCK // leaves), width)] * leaves,
            [room(sizes[0] // leaves, width)],
            cost,
            1 + len(levels),
            meta,
            *[all_rows[l] for l in levels],
            *quarters,
        )
        return to_leaves(picks)

    blocks = owned[0] // BLOCK
    quarters, top_parts = lax.optimization_barrier((quarters, top_parts))
    top, zero = jnp.zeros((blocks, leaves, thin, width), F32), jnp.uint32(0)
    for d, item in enumerate(top_parts):
        top = lax.dynamic_update_slice(top, item.reshape(blocks, 1, thin, width), (zero, leaf_index(1, d), zero, zero))
    results = [top.reshape(rhs[0].shape)]
    picks = picked([1], "pick_1", quarters, 0)
    chain, parts = [], []
    for l in (1, 2, 3):
        above = sum(sizes[1:l])
        keep, send, *chain = call(
            functools.partial(
                backward_panel_kernel,
                len(parts),
                leaves,
                helds[l],
                sizes[0] // BLOCK,
                helds[2] * listed[2] * thin if l == 3 else 0,
                len(chain),
            ),
            f"backward_panel_{l}",
            halves(chunks[l]) + ([shaped(above, width)] if l == 2 else []),
            ([room(above, width)] if l == 3 else [])
            + [
                room(panel[l].shape[1], width),
                pltpu.VMEM((panel[l].shape[1], 2 * width), BF16),
                room(spans[l], width),
            ],
            6 * panel[l].size * width,
            2,
            meta,
            own_rows[l],
            *picks,
            *parts,
            *chain,
            panel[l],
        )
        residue = solved[l] - scatter_sum(keep, send)
        if l == 1:
            picks = picked([2, 3], "pick_2_3", after(quarters, residue), BESIDE)
        x = call(
            backward_inv_kernel,
            f"backward_inv_{l}",
            shaped(helds[l], owned[l], width),
            [room(spans[l], width)],
            6 * inv[l].size * width,
            1,
            meta,
            *gather(residue),
            inv[l],
        )
        if l == 1:
            x, picks = lax.optimization_barrier((x, picks))
        x = leaf_sum(x, groups[l])
        if l < 3:
            parts = gather(x[0])
            placed = [x] + other_groups(beside(x, x), l)[1:]
            parts, placed = lax.optimization_barrier((parts, placed))
            results.append(place(placed, l))
    results.append(place(other_groups(x, 3), 3))
    return tuple(results)


def solution(mesh):
    across = P(None, "rows", None)
    return jax.shard_map(
        body,
        mesh=mesh,
        in_specs=(across,) * 4 + (P("rows", "leaf"),) * 4 + (P("leaf", "rows"),) * 3 + (P(None, "rows"),) * 3,
        out_specs=(across,) * 4,
        check_vma=False,
    )
```
